512 devices in a mesh: row: 64 (over z, x, core), col: 8 (over y).
Axes of the slice: x: 4, y: 8, z: 8, core: 2. Of those that a mesh axis runs over, the one named last changes fastest.
Arguments:
- front_in: float32 [32768, 4096], P('row', 'col')
- child_block: float32 [32768, 2048], P('row', 'col'), may hold values from -6 to 6
- child_rows: int32 [32768], P('row'), may hold values from 0 to 32767, as said below
- live_counts: int32 [64, 64], P('row'), may hold values from 0 to 8, as said below
- column_map: int32 [2048], P('col'), may hold values from 0 to 4095, as said below
Outputs:
- parent_front: float32 [32768, 4096], P('row', 'col')
- factor_rows: float32 [512, 4096], P(None, 'col')
The draws below stay inside these ranges and needn't reach their ends.
Inputs may be any that keep to these rules, and one draw needn't show every extreme that they name: `child_rows`: child row i of each row block (0 <= i < 512) goes to a parent row of row block i // 8, that is into rows (i // 8) * 512 to (i // 8 + 1) * 512 - 1; parent rows may repeat. Each row of live_counts holds both 0 and 8. `column_map`: the child columns held by column block c map to distinct parent columns of the same block, c * 512 to (c + 1) * 512 - 1.
All inputs are finite; a program needn't handle non-finite values.
Results may differ from the reference program's by a relative error of at most 0.00029.
Values sent between devices are 32-bit elements; how exact they have to be, the bound alone decides.
No kernel may reach another device: no remote copies, remote signals or barrier semaphores. Data moves between devices by JAX's collectives and lax.ppermute only.
A program may use at most 64 MiB of HBM per device.

```python
import math
import jax
import jax.numpy as jnp
from jax import lax

NC = 4096
PANEL = 256
CWIDTH = 2048
ROWS_DEV = 512
CAP = 8
OWNERS = 64
COLBLOCKS = 8
ROWS = 32768
CH_DEV = 512
CHROWS = 32768
COLS_DEV = 512
CW = 256


def draw_front_in(key, part):
    keys = jax.random.split(key, 3)
    row_scale = jnp.exp(jax.random.uniform(keys[1], (ROWS, 1), jnp.float32, math.log(0.3), math.log(3.0)))
    col_scale = jnp.exp(jax.random.uniform(keys[2], (1, NC), jnp.float32, math.log(0.3), math.log(3.0)))
    entries = jax.random.normal(keys[0], (ROWS, NC), jnp.float32)
    return (entries * row_scale * col_scale).astype(jnp.float32)


def draw_child_rows(key, part):
    row_index = jnp.arange(CHROWS, dtype=jnp.int32)
    owner_index = row_index % CH_DEV // CAP
    offsets = jax.random.randint(key, (CHROWS,), 0, ROWS_DEV, jnp.int32)
    offsets = jnp.where(row_index == CHROWS - 1, ROWS_DEV - 1, offsets)
    offsets = jnp.where(row_index == 0, 0, offsets)
    return (owner_index * ROWS_DEV + offsets).astype(jnp.int32)


def draw_live_counts(key, part):
    keys = jax.random.split(key, 3)
    single = jax.random.randint(keys[0], (OWNERS, OWNERS), 0, CAP + 1, jnp.int32)
    heated = jax.random.randint(keys[1], (1, OWNERS), 0, CAP + 1, jnp.int32)
    counts = (single + heated) // 2
    offset = jax.random.randint(keys[2], (), 0, OWNERS, jnp.int32)
    source = jnp.arange(OWNERS, dtype=jnp.int32)[:, None]
    target = jnp.arange(OWNERS, dtype=jnp.int32)[None, :]
    filled = target == (source * 5 + offset) % OWNERS
    emptied = target == (source * 5 + offset + 1) % OWNERS
    counts = jnp.where(filled, CAP, jnp.where(emptied, 0, counts))
    return counts.astype(jnp.int32)


def draw_column_map(key, part):

    def one_block(block_index):
        block_key = jax.random.fold_in(key, block_index)
        inner = jax.random.permutation(jax.random.fold_in(block_key, 1), COLS_DEV - 2)[:CW - 2].astype(jnp.int32) + 1
        ends = jnp.array([0, COLS_DEV - 1], dtype=jnp.int32)
        chosen = jax.random.permutation(jax.random.fold_in(block_key, 2), jnp.concatenate([ends, inner]))
        return chosen.astype(jnp.int32) + block_index * COLS_DEV
    blocks = jax.vmap(one_block)(jnp.arange(COLBLOCKS, dtype=jnp.int32))
    return blocks.reshape(CWIDTH).astype(jnp.int32)


def block_scale(key, dims, cuts, least, high):
    def one(dim, parts):
        draws = jax.random.uniform(jax.random.fold_in(jax.random.fold_in(key, 6), dim), (parts,), jnp.float32, least / len(cuts), high / len(cuts))
        return jnp.repeat(jnp.exp(draws), dims[dim] // parts).reshape((-1,) + (1,) * (len(dims) - dim - 1))

    gain = one(*cuts[0])
    for cut in cuts[1:]:
        gain = gain * one(*cut)
    return gain


def gaussian(stream_key, dims, width, most, cuts=(), kind=jnp.bfloat16):
    gain = block_scale(stream_key, dims, cuts, -0.22, 0.18) if cuts else 1.0
    values = jax.random.normal(stream_key, dims, jnp.float32) * width * gain
    return jnp.minimum(jnp.maximum(values, -most), most).astype(kind)


def setup_inputs(seed: int = 0) -> dict:
    arg_keys = jax.random.split(jax.random.key(seed), 6)
    return {
        "front_in": draw_front_in(jax.random.fold_in(arg_keys[5], 71), 0),
        "child_block": gaussian(arg_keys[1], (CHROWS, CWIDTH), 1.0, 6.0, ((0, 64), (1, 8)), jnp.float32),
        "child_rows": draw_child_rows(jax.random.fold_in(arg_keys[5], 71), 0),
        "live_counts": draw_live_counts(jax.random.fold_in(arg_keys[5], 71), 0),
        "column_map": draw_column_map(jax.random.fold_in(arg_keys[5], 71), 0),
    }


def reference(front_in, child_block, child_rows, live_counts, column_map):
    highest = lax.Precision.HIGHEST
    row_index = jnp.arange(CHROWS, dtype=jnp.int32)
    within = row_index % CH_DEV
    source = row_index // CH_DEV
    owner_index = within // CAP
    slot_index = within % CAP
    live_mask = (slot_index < live_counts[source, owner_index]).astype(jnp.float32)
    widened = jnp.zeros((CHROWS, NC), jnp.float32).at[:, column_map].add(child_block * live_mask[:, None])
    parent_front = front_in.at[child_rows].add(widened)
    root_rows = math.sqrt(ROWS)
    columns = jnp.arange(NC, dtype=jnp.int32)
    blocks = []
    for panel_index in range(2):
        first_col = panel_index * PANEL
        last_col = first_col + PANEL
        panel_cols = parent_front[:, first_col:last_col]
        gram_matrix = jnp.dot(panel_cols.T, panel_cols, precision=highest)
        lower_factor = jnp.linalg.cholesky(gram_matrix)
        basis_cols = jax.scipy.linalg.solve_triangular(lower_factor, panel_cols.T, lower=True).T
        product = jnp.dot(basis_cols.T, parent_front, precision=highest)
        coupled = jnp.where(columns[None, :] >= last_col, product, jnp.zeros_like(product))
        parent_front = parent_front - jnp.dot(basis_cols, coupled, precision=highest)
        parent_front = parent_front.at[:, first_col:last_col].set(basis_cols * root_rows)
        blocks.append(coupled.at[:, first_col:last_col].set(lower_factor.T) / root_rows)
    return (parent_front, jnp.concatenate(blocks, axis=0))
```

```python
import math

import jax
import jax.numpy as jnp
from jax import lax
from jax.experimental import pallas as pl
from jax.experimental.pallas import tpu as pltpu
from jax.sharding import Mesh, PartitionSpec as P

PANELS = 512
BLOCK = 128
SUB = 32
ROW = ("z", "x", "core")
VMEM = pl.BlockSpec(memory_space=pltpu.VMEM)


def dot(a, b, ca=1, cb=0):
    return lax.dot_general(
        a,
        b,
        (((ca,), (cb,)), ((), ())),
        precision=lax.Precision.HIGHEST,
        preferred_element_type=jnp.float32,
    )


def dot_fast(a, b, ca=1, cb=0):
    return lax.dot_general(
        a, b, (((ca,), (cb,)), ((), ())), preferred_element_type=jnp.float32
    )


def split3(a):
    hi = a.astype(jnp.bfloat16)
    rest = a - hi.astype(jnp.float32)
    mid = rest.astype(jnp.bfloat16)
    low = (rest - mid.astype(jnp.float32)).astype(jnp.bfloat16)
    return hi, mid, low


def call(kernel, out_shape, name, flops, *args):
    return pl.pallas_call(
        kernel,
        out_shape=out_shape,
        in_specs=[VMEM] * len(args),
        out_specs=jax.tree.map(lambda _: VMEM, out_shape),
        name=name,
        compiler_params=pltpu.CompilerParams(vmem_limit_bytes=24 << 20),
        cost_estimate=pl.CostEstimate(flops=flops, bytes_accessed=4 << 20, transcendentals=0),
    )(*args)


def f32(*shape):
    return jax.ShapeDtypeStruct(shape, jnp.float32)


def place_kernel(front_ref, arrived_ref, rows_ref, cols_ref, out_ref):
    height, width = front_ref.shape
    count, child_width = arrived_ref.shape
    col_hot = (
        lax.broadcasted_iota(jnp.int32, (width, child_width), 0) == cols_ref[...]
    ).astype(jnp.float32).astype(jnp.bfloat16)
    row_hot = (
        lax.broadcasted_iota(jnp.int32, (height, count), 0) == rows_ref[...]
    ).astype(jnp.float32).astype(jnp.bfloat16)
    total = front_ref[...]
    for term in split3(arrived_ref[...]):
        spread = dot_fast(term, col_hot, 1, 1).astype(jnp.bfloat16)
        total = total + dot_fast(row_hot, spread)
    out_ref[...] = total


def gram_kernel(a_ref, b_ref, out_ref):
    out_ref[...] = dot(a_ref[...], b_ref[...], 0, 0)


def factor_diagonal(block):
    done = []
    rest = block
    for sub in range(BLOCK // SUB):
        groups = [rest[8 * g : 8 * g + 8, :] for g in range(SUB // 8)]
        for j in range(SUB):
            column = SUB * sub + j
            own, at = divmod(j, 8)
            row = groups[own][at : at + 1, :]
            scale = lax.rsqrt(row[:, column : column + 1])
            scaled = row * scale
            for g in range(own, SUB // 8):
                factor = groups[g][:, column : column + 1] * scale
                updated = groups[g] - factor * scaled
                if g == own:
                    index = lax.broadcasted_iota(jnp.int32, updated.shape, 0)
                    kept = jnp.where(index == at, jnp.broadcast_to(scaled, updated.shape), groups[g])
                    updated = jnp.where(index > at, updated, kept)
                groups[g] = updated
        rows = jnp.concatenate(groups, axis=0)
        done.append(rows)
        if sub + 1 < BLOCK // SUB:
            rest = rest[SUB:, :] - dot(rows[:, SUB * (sub + 1) : BLOCK], rows, 0, 0)
    return jnp.concatenate(done, axis=0)


def eye(size):
    shape = (size, size)
    return (
        lax.broadcasted_iota(jnp.int32, shape, 0) == lax.broadcasted_iota(jnp.int32, shape, 1)
    ).astype(jnp.float32)


def factor_kernel(k, gram_ref, *refs):
    above, out_ref = refs[:-1], refs[-1]
    n = gram_ref.shape[0]
    rows = slice(k * BLOCK, (k + 1) * BLOCK)
    low, high = k * BLOCK, n + (k + 1) * BLOCK
    identity = eye(BLOCK)
    pad = [jnp.zeros((BLOCK, low), jnp.float32)] if k else []
    work = jnp.concatenate([gram_ref[rows, low:]] + pad + [identity], axis=1)
    for ref in above:
        work = work - dot(ref[:, rows], ref[:, low:high], 0, 0)
    diagonal = factor_diagonal(jnp.concatenate([work[:, :BLOCK], identity], axis=1))
    out_ref[:, low:high] = dot(diagonal[:, BLOCK:], work)
    out_ref[:, rows] = diagonal[:, :BLOCK]
    if k:
        out_ref[:, :low] = jnp.zeros((BLOCK, low), jnp.float32)
    if high < 2 * n:
        out_ref[:, high:] = jnp.zeros((BLOCK, 2 * n - high), jnp.float32)


def final_kernel(root_rows, front_ref, panel_ref, sums_ref, is_root_ref, *refs):
    blocks, (out_ref, factor_ref) = refs[:-2], refs[-2:]
    n = panel_ref.shape[1]
    inverse = jnp.concatenate([ref[:, n:] for ref in blocks], axis=0)
    basis = dot(panel_ref[...], inverse, 1, 1)
    coupled = dot(inverse, sums_ref[...])
    is_root = is_root_ref[0, 0] == 1
    out_ref[...] = jnp.where(
        is_root, basis * root_rows, front_ref[...] - dot(basis, coupled)
    )
    upper = jnp.concatenate([ref[:, :n] for ref in blocks], axis=0)
    factor_ref[...] = jnp.where(is_root, upper, coupled) * (1.0 / root_rows)


def exchange(blocks, axis):
    return lax.all_to_all(blocks, axis, split_axis=0, concat_axis=0, tiled=True)


def scatter_sum(x):
    for axis in ("core", "x", "z"):
        n = lax.axis_size(axis)
        x = jnp.sum(exchange(x.reshape(n, x.shape[0] // n, x.shape[1]), axis), axis=0)
    return x


def gathered(x, axis):
    n = lax.axis_size(axis)
    return exchange(jnp.broadcast_to(x[None], (n,) + x.shape), axis).reshape(
        n * x.shape[0], x.shape[1]
    )


def gather_rows(x):
    for axis in ("z", "x", "core"):
        x = gathered(x, axis)
    return x


def share_from_root(x):
    n = lax.axis_size("col")
    return exchange(x.reshape(n, x.shape[0] // n, x.shape[1]), "col")[0]


def on_device(front_in, child_block, child_rows, live_counts, column_map):
    rows_dev, cols_dev = front_in.shape
    owners = lax.axis_size(ROW)
    count, child_width = child_block.shape
    capacity = count // owners
    slots = jnp.arange(capacity, dtype=jnp.int32)
    live = slots[None, :] < live_counts[0][:, None]
    targets = jnp.where(live, child_rows.reshape(owners, capacity) % rows_dev, -1)
    arrived = exchange(child_block.reshape(owners, capacity, child_width), ROW)
    arrived_rows = exchange(targets.reshape(owners, 1, capacity), ROW)
    arrived = arrived.reshape(count, child_width)
    arrived_rows = arrived_rows.reshape(1, count)
    local_cols = (column_map % cols_dev).reshape(1, child_width)
    front = call(
        place_kernel, f32(rows_dev, cols_dev), "place", 2 << 30,
        front_in, arrived, arrived_rows, local_cols,
    )

    gram_part = call(gram_kernel, f32(PANELS, PANELS), "gram", 2 << 30, front, front)
    gram_share = scatter_sum(gram_part)
    gram_share = exchange(
        jnp.broadcast_to(gram_share[None], (lax.axis_size("col"),) + gram_share.shape), "col"
    )[0]
    gram = gather_rows(gram_share)

    panel = gathered(share_from_root(front), "col")
    sums = call(gram_kernel, f32(PANELS, cols_dev), "products", 2 << 30, panel, front)
    sums = gather_rows(scatter_sum(sums))

    blocks = []
    for k in range(PANELS // BLOCK):
        blocks.append(
            call(
                lambda *refs, k=k: factor_kernel(k, *refs),
                f32(BLOCK, 2 * PANELS), f"factor{k}", 10 << 30, gram, *blocks,
            )
        )

    is_root = (lax.axis_index("col") == 0).astype(jnp.int32).reshape(1, 1)
    return call(
        lambda *refs: final_kernel(math.sqrt(rows_dev * owners), *refs),
        (f32(rows_dev, cols_dev), f32(PANELS, cols_dev)), "final", 6 << 30,
        front, panel, sums, is_root, *blocks,
    )


def solution(mesh):
    row, col = mesh.shape["row"], mesh.shape["col"]
    fine = Mesh(mesh.devices.reshape(8, 4, row // 32, col), ROW + ("col",))
    return jax.shard_map(
        on_device,
        mesh=fine,
        in_specs=(P(ROW, "col"), P(ROW, "col"), P(ROW), P(ROW, None), P("col")),
        out_specs=(P(ROW, "col"), P(None, "col")),
        check_vma=False,
    )
```

```python
import math

import jax
import jax.numpy as jnp
from jax import lax
from jax.experimental import pallas as pl
from jax.experimental.pallas import tpu as pltpu
from jax.sharding import Mesh, PartitionSpec as P

PANELS = 512
BLOCK = 128
SUB = 32
ROW = ("z", "x", "core")
VMEM = pl.BlockSpec(memory_space=pltpu.VMEM)


def dot(a, b, ca=1, cb=0):
    return lax.dot_general(
        a,
        b,
        (((ca,), (cb,)), ((), ())),
        precision=lax.Precision.HIGHEST,
        preferred_element_type=jnp.float32,
    )


def dot_fast(a, b, ca=1, cb=0):
    return lax.dot_general(
        a, b, (((ca,), (cb,)), ((), ())), preferred_element_type=jnp.float32
    )


def split3(a):
    hi = a.astype(jnp.bfloat16)
    rest = a - hi.astype(jnp.float32)
    mid = rest.astype(jnp.bfloat16)
    low = (rest - mid.astype(jnp.float32)).astype(jnp.bfloat16)
    return hi, mid, low


def call(kernel, out_shape, name, flops, *args):
    return pl.pallas_call(
        kernel,
        out_shape=out_shape,
        in_specs=[VMEM] * len(args),
        out_specs=jax.tree.map(lambda _: VMEM, out_shape),
        name=name,
        compiler_params=pltpu.CompilerParams(vmem_limit_bytes=24 << 20),
        cost_estimate=pl.CostEstimate(flops=flops, bytes_accessed=4 << 20, transcendentals=0),
    )(*args)


def f32(*shape):
    return jax.ShapeDtypeStruct(shape, jnp.float32)


def place_kernel(front_ref, arrived_ref, cols_ref, out_ref):
    height, width = front_ref.shape
    count = arrived_ref.shape[0]
    child_width = cols_ref.shape[1]
    col_hot = (
        lax.broadcasted_iota(jnp.int32, (width, child_width), 0) == cols_ref[...]
    ).astype(jnp.float32).astype(jnp.bfloat16)
    targets = arrived_ref[:, child_width : child_width + 1].astype(jnp.int32)
    row_hot = (
        lax.broadcasted_iota(jnp.int32, (count, height), 1) == targets
    ).astype(jnp.float32).astype(jnp.bfloat16)
    total = front_ref[...]
    for term in split3(arrived_ref[:, :child_width]):
        spread = dot_fast(term, col_hot, 1, 1).astype(jnp.bfloat16)
        total = total + dot_fast(row_hot, spread, 0, 0)
    out_ref[...] = total


def gram_place(i, j):
    if i < 2:
        return (2 * j + i) * BLOCK
    return (2 * PANELS // BLOCK + 2 * (j - 2) + i - 2) * BLOCK


def gram_kernel(panel_ref, out_ref):
    half = PANELS // 2
    for first in range(2):
        cols = slice(half * first, PANELS)
        product = dot(panel_ref[:, half * first : half * (first + 1)], panel_ref[:, cols], 0, 0)
        for i in range(2):
            for j in range(2 * first, PANELS // BLOCK):
                at = gram_place(2 * first + i, j)
                left = (j - 2 * first) * BLOCK
                out_ref[at : at + BLOCK, :] = product[i * BLOCK : (i + 1) * BLOCK, left : left + BLOCK]


def product_kernel(a_ref, b_ref, out_ref):
    out_ref[...] = dot(a_ref[...], b_ref[...], 0, 0)


def factor_diagonal(block):
    done = []
    rest = block
    for sub in range(BLOCK // SUB):
        groups = [rest[8 * g : 8 * g + 8, :] for g in range(SUB // 8)]
        for j in range(SUB):
            column = SUB * sub + j
            own, at = divmod(j, 8)
            row = groups[own][at : at + 1, :]
            scale = lax.rsqrt(row[:, column : column + 1])
            scaled = row * scale
            for g in range(own, SUB // 8):
                factor = groups[g][:, column : column + 1] * scale
                updated = groups[g] - factor * scaled
                if g == own:
                    index = lax.broadcasted_iota(jnp.int32, updated.shape, 0)
                    kept = jnp.where(index == at, jnp.broadcast_to(scaled, updated.shape), groups[g])
                    updated = jnp.where(index > at, updated, kept)
                groups[g] = updated
        rows = jnp.concatenate(groups, axis=0)
        done.append(rows)
        if sub + 1 < BLOCK // SUB:
            rest = rest[SUB:, :] - dot(rows[:, SUB * (sub + 1) : BLOCK], rows, 0, 0)
    return jnp.concatenate(done, axis=0)


def eye(size):
    shape = (size, size)
    return (
        lax.broadcasted_iota(jnp.int32, shape, 0) == lax.broadcasted_iota(jnp.int32, shape, 1)
    ).astype(jnp.float32)


def factor_kernel(k, gram_ref, *refs):
    above, out_ref = refs[:-1], refs[-1]
    n = PANELS
    rows = slice(k * BLOCK, (k + 1) * BLOCK)
    low, high = k * BLOCK, n + (k + 1) * BLOCK
    identity = eye(BLOCK)
    pad = [jnp.zeros((BLOCK, low), jnp.float32)] if k else []
    starts = [gram_place(k, j) for j in range(k, n // BLOCK)]
    gram = [gram_ref[at : at + BLOCK, :] for at in starts]
    work = jnp.concatenate(gram + pad + [identity], axis=1)
    for ref in above:
        work = work - dot(ref[:, rows], ref[:, low:high], 0, 0)
    diagonal = factor_diagonal(jnp.concatenate([work[:, :BLOCK], identity], axis=1))
    out_ref[:, low:high] = dot(diagonal[:, BLOCK:], work)
    out_ref[:, rows] = diagonal[:, :BLOCK]
    if k:
        out_ref[:, :low] = jnp.zeros((BLOCK, low), jnp.float32)
    if high < 2 * n:
        out_ref[:, high:] = jnp.zeros((BLOCK, 2 * n - high), jnp.float32)


def final_kernel(root_rows, front_ref, panel_ref, sums_ref, is_root_ref, *refs):
    blocks, (out_ref, factor_ref) = refs[:-2], refs[-2:]
    n = panel_ref.shape[1]
    inverse = jnp.concatenate([ref[:, n:] for ref in blocks], axis=0)
    basis = dot(panel_ref[...], inverse, 1, 1)
    coupled = dot(inverse, sums_ref[...])
    is_root = is_root_ref[0, 0] == 1
    out_ref[...] = jnp.where(
        is_root, basis * root_rows, front_ref[...] - dot(basis, coupled)
    )
    upper = jnp.concatenate([ref[:, :n] for ref in blocks], axis=0)
    factor_ref[...] = jnp.where(is_root, upper, coupled) * (1.0 / root_rows)


def exchange(blocks, axis):
    return lax.all_to_all(blocks, axis, split_axis=0, concat_axis=0, tiled=True)


def scatter_sum(x):
    for axis, n in (("core", 2), (("z", "x"), 32)):
        x = jnp.sum(exchange(x.reshape(n, x.shape[0] // n, x.shape[1]), axis), axis=0)
    return x


def repeated(x, n):
    return jnp.broadcast_to(x[None], (n,) + x.shape)


def gather_rows(x):
    chips = lax.axis_size(("z", "x"))
    own = exchange(repeated(x, chips), ("z", "x")).reshape(chips * x.shape[0], x.shape[1])
    other = lax.ppermute(own, "core", [(0, 1), (1, 0)])
    return jnp.where(
        lax.axis_index("core") == 0,
        jnp.concatenate([own, other], axis=0),
        jnp.concatenate([other, own], axis=0),
    )


def from_root(x):
    n = lax.axis_size("col")
    shares = x.reshape(n, x.shape[0] // n, x.shape[1])
    mine = jnp.where(lax.axis_index("col") == 0, shares[0], 0.0)
    for k in range(1, n):
        mine = mine + lax.ppermute(shares[k], "col", [(0, k)])
    return lax.all_gather(mine, "col", tiled=True)


def on_device(front_in, child_block, child_rows, live_counts, column_map):
    rows_dev, cols_dev = front_in.shape
    owners = lax.axis_size(ROW)
    count, child_width = child_block.shape
    capacity = count // owners
    slots = jnp.arange(capacity, dtype=jnp.int32)
    live = slots[None, :] < live_counts[0][:, None]
    targets = jnp.where(live, child_rows.reshape(owners, capacity) % rows_dev, -1)
    sent = jnp.concatenate(
        [
            child_block.reshape(owners, capacity, child_width),
            jnp.broadcast_to(targets.astype(jnp.float32)[:, :, None], (owners, capacity, 128)),
        ],
        axis=2,
    )
    arrived = exchange(sent, ROW).reshape(count, child_width + 128)
    local_cols = (column_map % cols_dev).reshape(1, child_width)
    front = call(
        place_kernel, f32(rows_dev, cols_dev), "place", 2 << 30, front_in, arrived, local_cols
    )

    gram_part = call(gram_kernel, f32(3 * PANELS, BLOCK), "gram", 2 << 30, front)
    gram_share = scatter_sum(gram_part)
    gram_share = exchange(repeated(gram_share, lax.axis_size("col")), "col")[0]
    gram = gather_rows(gram_share)

    panel = from_root(front)
    sums = call(product_kernel, f32(PANELS, cols_dev), "products", 2 << 30, panel, front)
    sums = gather_rows(scatter_sum(sums))

    blocks = []
    for k in range(PANELS // BLOCK):
        blocks.append(
            call(
                lambda *refs, k=k: factor_kernel(k, *refs),
                f32(BLOCK, 2 * PANELS), f"factor{k}", 10 << 30, gram, *blocks,
            )
        )

    is_root = (lax.axis_index("col") == 0).astype(jnp.int32).reshape(1, 1)
    return call(
        lambda *refs: final_kernel(math.sqrt(rows_dev * owners), *refs),
        (f32(rows_dev, cols_dev), f32(PANELS, cols_dev)), "final", 6 << 30,
        front, panel, sums, is_root, *blocks,
    )


def solution(mesh):
    row, col = mesh.shape["row"], mesh.shape["col"]
    fine = Mesh(mesh.devices.reshape(8, 4, row // 32, col), ROW + ("col",))
    return jax.shard_map(
        on_device,
        mesh=fine,
        in_specs=(P(ROW, "col"), P(ROW, "col"), P(ROW), P(ROW, None), P("col")),
        out_specs=(P(ROW, "col"), P(None, "col")),
        check_vma=False,
    )
```

```python
import math

import jax
import jax.numpy as jnp
from jax import lax
from jax.experimental import pallas as pl
from jax.experimental.pallas import tpu as pltpu
from jax.sharding import Mesh, PartitionSpec as P

PANELS = 512
BLOCK = 128
SUB = 64
PIECES = 2
ROW = ("z", "x", "core")
VMEM = pl.BlockSpec(memory_space=pltpu.VMEM)
SMEM = pl.BlockSpec(memory_space=pltpu.SMEM)


def dot_fast(a, b, ca=1, cb=0):
    return lax.dot_general(
        a, b, (((ca,), (cb,)), ((), ())), preferred_element_type=jnp.float32
    )


def dot(a, b, ca=1, cb=0):
    return lax.dot_general(
        a,
        b,
        (((ca,), (cb,)), ((), ())),
        precision=lax.Precision.HIGHEST,
        preferred_element_type=jnp.float32,
    )


def split3(a):
    hi = a.astype(jnp.bfloat16)
    rest = a - hi.astype(jnp.float32)
    mid = rest.astype(jnp.bfloat16)
    low = (rest - mid.astype(jnp.float32)).astype(jnp.bfloat16)
    return hi, mid, low


def f32(*shape):
    return jax.ShapeDtypeStruct(shape, jnp.float32)


def call(kernel, out_shape, name, flops, *args, scalars=(), scratch=()):
    return pl.pallas_call(
        kernel,
        out_shape=out_shape,
        in_specs=[SMEM] * len(scalars) + [VMEM] * len(args),
        out_specs=jax.tree.map(lambda _: VMEM, out_shape),
        scratch_shapes=scratch,
        name=name,
        compiler_params=pltpu.CompilerParams(vmem_limit_bytes=14 << 20),
        cost_estimate=pl.CostEstimate(flops=flops, bytes_accessed=4 << 20, transcendentals=0),
    )(*[s.reshape(1, 1) for s in scalars], *args)


def iota(shape, axis):
    return lax.broadcasted_iota(jnp.int32, shape, axis)


def hot(mask):
    return mask.astype(jnp.float32).astype(jnp.bfloat16)


def eye(size):
    return (iota((size, size), 0) == iota((size, size), 1)).astype(jnp.float32)


def pack_kernel(height, capacity, child_ref, rows_ref, live_ref, out_ref):
    count, width = child_ref.shape
    owners = live_ref.shape[1]
    lanes = rows_ref.shape[1]
    out_ref[:, :width] = child_ref[...]
    live = jnp.broadcast_to(live_ref[...].astype(jnp.float32), (count, owners))
    owner = lax.div(iota((count, owners), 0), jnp.int32(capacity))
    live = jnp.sum(jnp.where(owner == iota((count, owners), 1), live, 0.0), axis=1, keepdims=True)
    slot = lax.rem(iota((count, 1), 0), jnp.int32(capacity)).astype(jnp.float32)
    local = lax.rem(rows_ref[...], jnp.int32(height)).astype(jnp.float32)
    identity = eye(lanes)
    rows = jnp.concatenate(
        [
            jnp.sum(jnp.broadcast_to(local[g : g + 1, :], (lanes, lanes)) * identity, axis=1, keepdims=True)
            for g in range(count // lanes)
        ],
        axis=0,
    )
    targets = jnp.where(slot < live, rows, -1.0)
    out_ref[:, width:] = jnp.broadcast_to(targets, (count, BLOCK))


def placed(front, rows, targets, cols):
    height, width = front.shape
    count, child_width = rows.shape
    col_hot = hot(iota((width, child_width), 0) == cols)
    row_hot = hot(iota((count, height), 1) == targets)
    total = front
    for term in split3(rows):
        spread = dot_fast(term, col_hot, 1, 1).astype(jnp.bfloat16)
        total = total + dot_fast(row_hot, spread, 0, 0)
    return total


def place_kernel(front_ref, arrived_ref, cols_ref, out_ref, shares_ref):
    child_width = cols_ref.shape[1]
    rows = arrived_ref[:, :child_width]
    targets = arrived_ref[:, child_width : child_width + 1].astype(jnp.int32)
    out_ref[...] = placed(front_ref[...], rows, targets, cols_ref[...])
    parts, height = shares_ref.shape[0], shares_ref.shape[1] // 2
    for k in range(parts):
        for h in range(2):
            shares_ref[k, h * height : (h + 1) * height, :] = rows[
                k * height : (k + 1) * height, h * BLOCK : (h + 1) * BLOCK
            ]


def place_panel_kernel(front_ref, shares_ref, cols_ref, arrived_ref, out_ref):
    parts, height = shares_ref.shape[0], shares_ref.shape[1] // 2
    child_width = 2 * BLOCK
    rows = jnp.concatenate(
        [
            jnp.concatenate([shares_ref[k, :height, :], shares_ref[k, height:, :]], axis=1)
            for k in range(parts)
        ],
        axis=0,
    )
    cols = jnp.concatenate([cols_ref[0:1, :], cols_ref[1:2, :]], axis=1).astype(jnp.int32)
    targets = arrived_ref[:, child_width : child_width + 1].astype(jnp.int32)
    out_ref[...] = placed(front_ref[...], rows, targets, cols)


def halves(core_ref, whole_ref, keep_ref, send_ref):
    height = keep_ref.shape[0]
    core = core_ref[0, 0]
    keep_ref[...] = whole_ref[pl.ds(pl.multiple_of(core * height, height), height), :]
    send_ref[...] = whole_ref[pl.ds(pl.multiple_of((1 - core) * height, height), height), :]


def gram_place(i, j):
    if i < 2:
        return (2 * j + i) * BLOCK
    return (2 * PANELS // BLOCK + 2 * (j - 2) + i - 2) * BLOCK


def gram_kernel(core_ref, panel_ref, keep_ref, send_ref, whole_ref):
    half = PANELS // 2
    for first in range(2):
        cols = slice(half * first, PANELS)
        product = dot(panel_ref[:, half * first : half * (first + 1)], panel_ref[:, cols], 0, 0)
        for i in range(2):
            for j in range(2 * first, PANELS // BLOCK):
                at = gram_place(2 * first + i, j)
                left = (j - 2 * first) * BLOCK
                whole_ref[at : at + BLOCK, :] = product[i * BLOCK : (i + 1) * BLOCK, left : left + BLOCK]
    halves(core_ref, whole_ref, keep_ref, send_ref)


def product_kernel(core_ref, panel_ref, front_ref, keep_ref, send_ref, whole_ref):
    whole_ref[...] = dot(panel_ref[...], front_ref[...], 0, 0)
    halves(core_ref, whole_ref, keep_ref, send_ref)


def factor_diagonal(block):
    width = block.shape[1]
    done = []
    rest = block
    at_narrow, at_wide = iota((8, BLOCK), 0), iota((8, width), 0)
    count = SUB // 8
    for sub in range(BLOCK // SUB):
        groups = [rest[8 * g : 8 * g + 8, :] for g in range(count)]
        for p in range(count):
            first = SUB * sub + 8 * p
            spread = {
                (g, k): jnp.broadcast_to(groups[g][:, first + k : first + k + 1], (8, BLOCK))
                for g in range(p, count)
                for k in range(8)
            }
            for j in range(8):
                scale = lax.rsqrt(jnp.broadcast_to(spread[p, j][j : j + 1, :], (8, BLOCK)))
                factor = {g: spread[g, j] * scale for g in range(p, count)}
                factor[p] = jnp.where(at_narrow > j, factor[p], 0.0)
                for k in range(j + 1, 8):
                    pivot = jnp.broadcast_to(spread[p, k][j : j + 1, :], (8, BLOCK)) * scale
                    for g in range(p, count):
                        spread[g, k] = spread[g, k] - factor[g] * pivot
                wide = jnp.concatenate([scale] * (width // BLOCK), axis=1)
                row = jnp.broadcast_to(groups[p][j : j + 1, :], (8, width)) * wide
                for g in range(p, count):
                    updated = groups[g] - jnp.concatenate([factor[g]] * (width // BLOCK), axis=1) * row
                    groups[g] = jnp.where(at_wide == j, row, updated) if g == p else updated
        rows = jnp.concatenate(groups, axis=0)
        done.append(rows)
        if sub + 1 < BLOCK // SUB:
            rest = rest[SUB:, :] - dot(rows[:, SUB * (sub + 1) : BLOCK], rows, 0, 0)
    return jnp.concatenate(done, axis=0)


def in_order(core_ref, own, other):
    first = core_ref[0, 0] == 0
    return jnp.concatenate(
        [jnp.where(first, own, other), jnp.where(first, other, own)], axis=0
    )


def factor_kernel(piece, core_ref, own_ref, other_ref, *refs):
    above, out_ref = refs[:-1], refs[-1]
    n = PANELS
    per = n // BLOCK // PIECES
    gram = in_order(core_ref, own_ref[...], other_ref[...])
    identity = eye(BLOCK)

    def rows_of(block):
        at = block % per * BLOCK
        return (*above, out_ref)[block // per], slice(at, at + BLOCK)

    for k in range(piece * per, (piece + 1) * per):
        _, rows = rows_of(k)
        low, high = k * BLOCK, n + (k + 1) * BLOCK
        starts = [gram_place(k, j) for j in range(k, n // BLOCK)]
        pad = [jnp.zeros((BLOCK, low), jnp.float32)] if k else []
        work = jnp.concatenate([gram[at : at + BLOCK, :] for at in starts] + pad + [identity], axis=1)
        for upper in range(k):
            ref, at = rows_of(upper)
            work = work - dot(ref[at, low : low + BLOCK], ref[at, low:high], 0, 0)
        diagonal = factor_diagonal(jnp.concatenate([work[:, :BLOCK], identity], axis=1))
        out_ref[rows, low:high] = dot(diagonal[:, BLOCK:], work)
        out_ref[rows, low : low + BLOCK] = diagonal[:, :BLOCK]
        if k:
            out_ref[rows, :low] = jnp.zeros((BLOCK, low), jnp.float32)
        if high < 2 * n:
            out_ref[rows, high:] = jnp.zeros((BLOCK, 2 * n - high), jnp.float32)


def inverse_rows(blocks, i):
    per = blocks[0].shape[0]
    ref, at = blocks[i * BLOCK // per], i * BLOCK % per
    return ref[at : at + BLOCK, PANELS : PANELS + (i + 1) * BLOCK]


def basis_kernel(panel_ref, *refs):
    blocks, out_ref = refs[:-1], refs[-1]
    for i in range(PANELS // BLOCK):
        upto = (i + 1) * BLOCK
        out_ref[:, i * BLOCK : upto] = dot(panel_ref[:, :upto], inverse_rows(blocks, i), 1, 1)


def final_kernel(root_rows, core_ref, root_ref, front_ref, basis_ref, own_ref, other_ref, *refs):
    blocks, (out_ref, factor_ref) = refs[:-2], refs[-2:]
    sums = in_order(core_ref, own_ref[...], other_ref[...])
    coupled = jnp.concatenate(
        [dot(inverse_rows(blocks, i), sums[: (i + 1) * BLOCK, :]) for i in range(PANELS // BLOCK)],
        axis=0,
    )
    is_root = root_ref[0, 0] == 1
    basis = basis_ref[...]
    basis_hi, basis_mid, _ = split3(basis)
    coupled_hi, coupled_mid, _ = split3(coupled)
    update = dot_fast(basis_mid, coupled_hi) + dot_fast(basis_hi, coupled_mid)
    update = update + dot_fast(basis_hi, coupled_hi)
    out_ref[...] = jnp.where(is_root, basis * root_rows, front_ref[...] - update)
    upper = jnp.concatenate([ref[:, :PANELS] for ref in blocks], axis=0)
    factor_ref[...] = jnp.where(is_root, upper, coupled) * (1.0 / root_rows)


def exchange(blocks, axis):
    return lax.all_to_all(blocks, axis, split_axis=0, concat_axis=0, tiled=True)


def repeated(x, n):
    return jnp.broadcast_to(x[None], (n,) + x.shape)


def swapped(x):
    return lax.ppermute(x, "core", [(0, 1), (1, 0)])


def chip_share(x):
    n = lax.axis_size(("z", "x"))
    return jnp.sum(exchange(x.reshape(n, x.shape[0] // n, x.shape[1]), ("z", "x")), axis=0)


def all_shares(x):
    n = lax.axis_size(("z", "x"))
    return exchange(repeated(x, n), ("z", "x")).reshape(n * x.shape[0], x.shape[1])


def share_of_root(shares):
    mine = jnp.where(lax.axis_index("col") == 0, shares[0], 0.0)
    for k in range(1, lax.axis_size("col")):
        mine = mine + lax.ppermute(shares[k], "col", [(0, k)])
    return mine


def on_device(front_in, child_block, child_rows, live_counts, column_map):
    rows_dev, cols_dev = front_in.shape
    owners, parts = lax.axis_size(ROW), lax.axis_size("col")
    count, child_width = child_block.shape
    capacity = count // owners
    core = lax.axis_index("core").astype(jnp.int32)
    is_root = (lax.axis_index("col") == 0).astype(jnp.int32)
    halved = (f32(3 * PANELS // 2, BLOCK),) * 2
    local_cols = column_map % cols_dev

    sent = call(
        lambda *refs: pack_kernel(rows_dev, capacity, *refs),
        f32(count, child_width + BLOCK), "pack", 1 << 20,
        child_block, child_rows.reshape(count // BLOCK, BLOCK), live_counts,
    )
    arrived = exchange(sent.reshape(owners, capacity, child_width + BLOCK), ROW)
    arrived = arrived.reshape(count, child_width + BLOCK)
    front_share = share_of_root(front_in.reshape(parts, rows_dev // parts, cols_dev))
    arrived, front_share = lax.optimization_barrier((arrived, front_share))
    panel_front = lax.all_gather(front_share, "col", tiled=True)

    front, shares = call(
        place_kernel, (f32(rows_dev, cols_dev), f32(parts, 2 * count // parts, BLOCK)),
        "place", 2 << 30, front_in, arrived, local_cols.reshape(1, child_width),
    )
    keep, send = call(
        gram_kernel, halved, "gram", 2 << 30, front, scalars=(core,),
        scratch=[pltpu.VMEM((3 * PANELS, BLOCK), jnp.float32)],
    )
    half, shares = lax.optimization_barrier((keep + swapped(send), shares))
    gram_share = chip_share(half)

    rows_of_share = 2 * count // parts
    to_all = jnp.concatenate(
        [
            share_of_root(shares),
            gram_share,
            local_cols.astype(jnp.float32).reshape(child_width // BLOCK, BLOCK),
            jnp.zeros((8 - child_width // BLOCK, BLOCK), jnp.float32),
        ],
        axis=0,
    )
    from_all = exchange(repeated(to_all, parts), "col")
    gram_end = rows_of_share + gram_share.shape[0]
    own_gram = all_shares(from_all[0, rows_of_share:gram_end])
    other_gram = swapped(own_gram)

    panel = call(
        place_panel_kernel, f32(rows_dev, PANELS), "place_panel", 2 << 30,
        panel_front, from_all[:, :rows_of_share], from_all[0, gram_end:], arrived,
    )
    keep, send = call(
        product_kernel, (f32(PANELS // 2, cols_dev),) * 2, "products", 2 << 30, panel, front,
        scalars=(core,), scratch=[pltpu.VMEM((PANELS, cols_dev), jnp.float32)],
    )
    sums_share = chip_share(keep + swapped(send))

    blocks = []
    for piece in range(PIECES):
        blocks.append(
            call(
                lambda *refs, piece=piece: factor_kernel(piece, *refs),
                f32(PANELS // PIECES, 2 * PANELS), f"factor{piece}", 10 << 30,
                own_gram, other_gram, *blocks, scalars=(core,),
            )
        )
        if piece == 0:
            sums_share, blocks[0] = lax.optimization_barrier((sums_share, blocks[0]))
            own_sums = all_shares(sums_share)
    own_sums, blocks[1] = lax.optimization_barrier((own_sums, blocks[1]))
    other_sums = swapped(own_sums)
    basis = call(basis_kernel, f32(rows_dev, PANELS), "basis", 2 << 30, panel, *blocks)
    return call(
        lambda *refs: final_kernel(math.sqrt(rows_dev * owners), *refs),
        (f32(rows_dev, cols_dev), f32(PANELS, cols_dev)), "final", 4 << 30,
        front, basis, own_sums, other_sums, *blocks, scalars=(core, is_root),
    )


def solution(mesh):
    row, col = mesh.shape["row"], mesh.shape["col"]
    fine = Mesh(mesh.devices.reshape(8, 4, row // 32, col), ROW + ("col",))
    return jax.shard_map(
        on_device,
        mesh=fine,
        in_specs=(P(ROW, "col"), P(ROW, "col"), P(ROW), P(ROW, None), P("col")),
        out_specs=(P(ROW, "col"), P(None, "col")),
        check_vma=False,
    )
```

```python
import math

import jax
import jax.numpy as jnp
from jax import lax
from jax.experimental import pallas as pl
from jax.experimental.pallas import tpu as pltpu
from jax.sharding import Mesh, PartitionSpec as P

PANELS = 512
BLOCK = 128
SUB = 64
PIECES = 2
ROW = ("z", "x", "core")
VMEM = pl.BlockSpec(memory_space=pltpu.VMEM)
SMEM = pl.BlockSpec(memory_space=pltpu.SMEM)


def dot_fast(a, b, ca=1, cb=0):
    return lax.dot_general(
        a, b, (((ca,), (cb,)), ((), ())), preferred_element_type=jnp.float32
    )


def dot(a, b, ca=1, cb=0):
    return lax.dot_general(
        a,
        b,
        (((ca,), (cb,)), ((), ())),
        precision=lax.Precision.HIGHEST,
        preferred_element_type=jnp.float32,
    )


def split3(a):
    hi = a.astype(jnp.bfloat16)
    rest = a - hi.astype(jnp.float32)
    mid = rest.astype(jnp.bfloat16)
    low = (rest - mid.astype(jnp.float32)).astype(jnp.bfloat16)
    return hi, mid, low


def f32(*shape):
    return jax.ShapeDtypeStruct(shape, jnp.float32)


def call(kernel, out_shape, name, flops, *args, scalars=(), scratch=(), vmem=14):
    return pl.pallas_call(
        kernel,
        out_shape=out_shape,
        in_specs=[SMEM] * len(scalars) + [VMEM] * len(args),
        out_specs=jax.tree.map(lambda _: VMEM, out_shape),
        scratch_shapes=scratch,
        name=name,
        compiler_params=pltpu.CompilerParams(vmem_limit_bytes=vmem << 20),
        cost_estimate=pl.CostEstimate(flops=flops, bytes_accessed=4 << 20, transcendentals=0),
    )(*[s.reshape(1, 1) for s in scalars], *args)


def iota(shape, axis):
    return lax.broadcasted_iota(jnp.int32, shape, axis)


def hot(mask):
    return mask.astype(jnp.float32).astype(jnp.bfloat16)


def eye(size):
    return (iota((size, size), 0) == iota((size, size), 1)).astype(jnp.float32)


def pack_kernel(height, capacity, child_ref, rows_ref, live_ref, out_ref):
    count, width = child_ref.shape
    owners = live_ref.shape[1]
    lanes = rows_ref.shape[1]
    out_ref[:, :width] = child_ref[...]
    live = jnp.broadcast_to(live_ref[...].astype(jnp.float32), (count, owners))
    owner = lax.div(iota((count, owners), 0), jnp.int32(capacity))
    live = jnp.sum(jnp.where(owner == iota((count, owners), 1), live, 0.0), axis=1, keepdims=True)
    slot = lax.rem(iota((count, 1), 0), jnp.int32(capacity)).astype(jnp.float32)
    local = lax.rem(rows_ref[...], jnp.int32(height)).astype(jnp.float32)
    identity = eye(lanes)
    rows = jnp.concatenate(
        [
            jnp.sum(jnp.broadcast_to(local[g : g + 1, :], (lanes, lanes)) * identity, axis=1, keepdims=True)
            for g in range(count // lanes)
        ],
        axis=0,
    )
    targets = jnp.where(slot < live, rows, -1.0)
    out_ref[:, width:] = jnp.broadcast_to(targets, (count, BLOCK))


def placed(front, rows, targets, cols):
    height, width = front.shape
    count, child_width = rows.shape
    col_hot = hot(iota((width, child_width), 0) == cols)
    row_hot = hot(iota((count, height), 1) == targets)
    total = front
    for term in split3(rows):
        spread = dot_fast(term, col_hot, 1, 1).astype(jnp.bfloat16)
        total = total + dot_fast(row_hot, spread, 0, 0)
    return total


def choose_kernel(root_ref, own_ref, *refs):
    arrived, out_ref = refs[:-1], refs[-1]
    total = arrived[0][...]
    for ref in arrived[1:]:
        total = total + ref[...]
    out_ref[...] = jnp.where(root_ref[0, 0] == 1, own_ref[...], total)


def add_kernel(a_ref, b_ref, out_ref):
    out_ref[...] = a_ref[...] + b_ref[...]


def fold_kernel(x_ref, out_ref):
    terms = [x_ref[i] for i in range(x_ref.shape[0])]
    while len(terms) > 1:
        terms = [a + b for a, b in zip(terms[::2], terms[1::2])]
    for i in range(out_ref.shape[0]):
        out_ref[i] = terms[0]


def first_kernel(x_ref, out_ref):
    for i in range(out_ref.shape[0]):
        out_ref[i] = x_ref[0]


def halves(core_ref, whole_ref, keep_ref, send_ref):
    height = keep_ref.shape[0]
    core = core_ref[0, 0]
    keep_ref[...] = whole_ref[pl.ds(pl.multiple_of(core * height, height), height), :]
    send_ref[...] = whole_ref[pl.ds(pl.multiple_of((1 - core) * height, height), height), :]


def gram_place(i, j):
    if i < 2:
        return (2 * j + i) * BLOCK
    return (2 * PANELS // BLOCK + 2 * (j - 2) + i - 2) * BLOCK


def place_kernel(
    core_ref, front_ref, arrived_ref, cols_ref, out_ref, keep_ref, send_ref, *refs
):
    share_refs, whole_ref = refs[:-1], refs[-1]
    child_width = cols_ref.shape[1]
    targets = arrived_ref[:, child_width : child_width + 1].astype(jnp.int32)
    front = placed(front_ref[...], arrived_ref[:, :child_width], targets, cols_ref[...])
    out_ref[...] = front
    height = share_refs[0].shape[0]
    for k, ref in enumerate(share_refs):
        ref[...] = front[k * height : (k + 1) * height, :]
    half = PANELS // 2
    for first in range(2):
        cols = slice(half * first, PANELS)
        product = dot(front[:, half * first : half * (first + 1)], front[:, cols], 0, 0)
        for i in range(2):
            for j in range(2 * first, PANELS // BLOCK):
                at = gram_place(2 * first + i, j)
                left = (j - 2 * first) * BLOCK
                whole_ref[at : at + BLOCK, :] = product[i * BLOCK : (i + 1) * BLOCK, left : left + BLOCK]
    halves(core_ref, whole_ref, keep_ref, send_ref)


def product_kernel(core_ref, panel_ref, front_ref, keep_ref, send_ref, whole_ref):
    whole_ref[...] = dot(panel_ref[...], front_ref[...], 0, 0)
    halves(core_ref, whole_ref, keep_ref, send_ref)


def factor_diagonal(block):
    width = block.shape[1]
    done = []
    rest = block
    at_narrow, at_wide = iota((8, BLOCK), 0), iota((8, width), 0)
    count = SUB // 8
    for sub in range(BLOCK // SUB):
        groups = [rest[8 * g : 8 * g + 8, :] for g in range(count)]
        for p in range(count):
            first = SUB * sub + 8 * p
            spread = {
                (g, k): jnp.broadcast_to(groups[g][:, first + k : first + k + 1], (8, BLOCK))
                for g in range(p, count)
                for k in range(8)
            }
            for j in range(8):
                scale = lax.rsqrt(jnp.broadcast_to(spread[p, j][j : j + 1, :], (8, BLOCK)))
                factor = {g: spread[g, j] * scale for g in range(p, count)}
                factor[p] = jnp.where(at_narrow > j, factor[p], 0.0)
                for k in range(j + 1, 8):
                    pivot = jnp.broadcast_to(spread[p, k][j : j + 1, :], (8, BLOCK)) * scale
                    for g in range(p, count):
                        spread[g, k] = spread[g, k] - factor[g] * pivot
                wide = jnp.concatenate([scale] * (width // BLOCK), axis=1)
                row = jnp.broadcast_to(groups[p][j : j + 1, :], (8, width)) * wide
                for g in range(p, count):
                    updated = groups[g] - jnp.concatenate([factor[g]] * (width // BLOCK), axis=1) * row
                    groups[g] = jnp.where(at_wide == j, row, updated) if g == p else updated
        rows = jnp.concatenate(groups, axis=0)
        done.append(rows)
        if sub + 1 < BLOCK // SUB:
            rest = rest[SUB:, :] - dot(rows[:, SUB * (sub + 1) : BLOCK], rows, 0, 0)
    return jnp.concatenate(done, axis=0)


def in_order(core_ref, own, other):
    first = core_ref[0, 0] == 0
    return jnp.concatenate(
        [jnp.where(first, own, other), jnp.where(first, other, own)], axis=0
    )


def factor_kernel(piece, core_ref, own_ref, other_ref, *refs):
    above, out_ref = refs[:-1], refs[-1]
    n = PANELS
    per = n // BLOCK // PIECES
    gram = in_order(core_ref, own_ref[...], other_ref[...])
    identity = eye(BLOCK)

    def rows_of(block):
        at = block % per * BLOCK
        start = block // per * per * BLOCK
        return (*above, out_ref)[block // per], slice(at, at + BLOCK), start

    for k in range(piece * per, (piece + 1) * per):
        _, rows, start = rows_of(k)
        low, high = k * BLOCK, n + (k + 1) * BLOCK
        starts = [gram_place(k, j) for j in range(k, n // BLOCK)]
        pad = [jnp.zeros((BLOCK, low), jnp.float32)] if k else []
        work = jnp.concatenate([gram[at : at + BLOCK, :] for at in starts] + pad + [identity], axis=1)
        for upper in range(k):
            ref, at, shift = rows_of(upper)
            end = min(high, shift + ref.shape[1])
            factor = dot(ref[at, low - shift : low - shift + BLOCK], ref[at, low - shift : end - shift], 0, 0)
            if end < high:
                factor = jnp.concatenate([factor, jnp.zeros((BLOCK, high - end), jnp.float32)], axis=1)
            work = work - factor
        diagonal = factor_diagonal(jnp.concatenate([work[:, :BLOCK], identity], axis=1))
        out_ref[rows, low - start : high - start] = dot(diagonal[:, BLOCK:], work)
        out_ref[rows, low - start : low - start + BLOCK] = diagonal[:, :BLOCK]
        if low > start:
            out_ref[rows, : low - start] = jnp.zeros((BLOCK, low - start), jnp.float32)
        if high - start < out_ref.shape[1]:
            out_ref[rows, high - start :] = jnp.zeros((BLOCK, out_ref.shape[1] - high + start), jnp.float32)


def inverse_rows(blocks, i):
    per = blocks[0].shape[0]
    ref, at = blocks[i * BLOCK // per], i * BLOCK % per
    left = PANELS - i * BLOCK // per * per
    return ref[at : at + BLOCK, left : left + (i + 1) * BLOCK]


def basis_kernel(panel_ref, *refs):
    blocks, out_ref = refs[:-1], refs[-1]
    for i in range(PANELS // BLOCK):
        upto = (i + 1) * BLOCK
        out_ref[:, i * BLOCK : upto] = dot(panel_ref[:, :upto], inverse_rows(blocks, i), 1, 1)


def final_kernel(root_rows, core_ref, root_ref, front_ref, basis_ref, own_ref, other_ref, *refs):
    blocks, (out_ref, factor_ref) = refs[:-2], refs[-2:]
    sums = in_order(core_ref, own_ref[...], other_ref[...])
    coupled = jnp.concatenate(
        [dot(inverse_rows(blocks, i), sums[: (i + 1) * BLOCK, :]) for i in range(PANELS // BLOCK)],
        axis=0,
    )
    is_root = root_ref[0, 0] == 1
    basis = basis_ref[...]
    basis_hi, basis_mid, _ = split3(basis)
    coupled_hi, coupled_mid, _ = split3(coupled)
    update = dot_fast(basis_mid, coupled_hi) + dot_fast(basis_hi, coupled_mid)
    update = update + dot_fast(basis_hi, coupled_hi)
    out_ref[...] = jnp.where(is_root, basis * root_rows, front_ref[...] - update)
    per = PANELS // PIECES
    upper = jnp.concatenate(
        [
            jnp.concatenate(
                ([jnp.zeros((per, at), jnp.float32)] if at else []) + [ref[:, : PANELS - at]], axis=1
            )
            for ref, at in zip(blocks, range(0, PANELS, per))
        ],
        axis=0,
    )
    factor_ref[...] = jnp.where(is_root, upper, coupled) * (1.0 / root_rows)


def exchange(blocks, axis):
    return lax.all_to_all(blocks, axis, split_axis=0, concat_axis=0, tiled=True)


def swapped(x):
    return lax.ppermute(x, "core", [(0, 1), (1, 0)])


def summed(a, b):
    return call(add_kernel, f32(*a.shape), "add", 1 << 20, a, b, vmem=4)


def split_rows(x, n):
    return x.reshape(n, x.shape[0] // n, x.shape[1])


def merge_rows(x):
    return x.reshape(x.shape[0] * x.shape[1], x.shape[2])


def folded(x, n):
    return call(fold_kernel, f32(n, *x.shape[1:]), "fold", 1 << 20, x, vmem=6)


def on_device(front_in, child_block, child_rows, live_counts, column_map):
    rows_dev, cols_dev = front_in.shape
    owners, parts = lax.axis_size(ROW), lax.axis_size("col")
    chips = lax.axis_size(("z", "x"))
    count, child_width = child_block.shape
    capacity = count // owners
    core = lax.axis_index("core").astype(jnp.int32)
    is_root = (lax.axis_index("col") == 0).astype(jnp.int32)
    halved = (f32(3 * PANELS // 2, BLOCK),) * 2
    local_cols = column_map % cols_dev

    sent = call(
        lambda *refs: pack_kernel(rows_dev, capacity, *refs),
        f32(count, child_width + BLOCK), "pack", 1 << 20,
        child_block, child_rows.reshape(count // BLOCK, BLOCK), live_counts,
    )
    arrived = merge_rows(exchange(sent.reshape(owners, capacity, child_width + BLOCK), ROW))

    share = f32(rows_dev // parts, cols_dev)
    front, keep, send, *shares = call(
        place_kernel, [f32(rows_dev, cols_dev), *halved] + [share] * parts,
        "place", 4 << 30, front_in, arrived, local_cols.reshape(1, child_width), scalars=(core,),
        scratch=[pltpu.VMEM((3 * PANELS, BLOCK), jnp.float32)],
    )
    sent_shares = [lax.ppermute(shares[k], "col", [(0, k)]) for k in range(1, parts)]
    panel_share = call(
        choose_kernel, share, "choose", 1 << 20, shares[0], *sent_shares, scalars=(is_root,), vmem=4
    )
    panel = lax.all_gather(panel_share, "col", tiled=True)

    half = summed(keep, swapped(send))
    gram_share = folded(exchange(split_rows(half, chips), ("z", "x")), parts)
    gram_share = exchange(gram_share, "col")
    gram_share = call(
        first_kernel, f32(chips, *gram_share.shape[1:]), "first", 1 << 20, gram_share, vmem=4
    )
    own_gram = merge_rows(exchange(gram_share, ("z", "x")))
    other_gram = swapped(own_gram)

    keep, send = call(
        product_kernel, (f32(PANELS // 2, cols_dev),) * 2, "products", 2 << 30, panel, front,
        scalars=(core,), scratch=[pltpu.VMEM((PANELS, cols_dev), jnp.float32)],
    )
    half = summed(keep, swapped(send))
    sums_share = folded(exchange(split_rows(half, chips), ("z", "x")), chips)

    blocks = []
    for piece in range(PIECES):
        blocks.append(
            call(
                lambda *refs, piece=piece: factor_kernel(piece, *refs),
                f32(PANELS // PIECES, 3 * PANELS // 2), f"factor{piece}", 10 << 30,
                own_gram, other_gram, *blocks, scalars=(core,),
            )
        )
        if piece == 0:
            sums_share, blocks[0] = lax.optimization_barrier((sums_share, blocks[0]))
            own_sums = merge_rows(exchange(sums_share, ("z", "x")))
    own_sums, blocks[1] = lax.optimization_barrier((own_sums, blocks[1]))
    other_sums = swapped(own_sums)
    basis = call(basis_kernel, f32(rows_dev, PANELS), "basis", 2 << 30, panel, *blocks)
    return call(
        lambda *refs: final_kernel(math.sqrt(rows_dev * owners), *refs),
        (f32(rows_dev, cols_dev), f32(PANELS, cols_dev)), "final", 4 << 30,
        front, basis, own_sums, other_sums, *blocks, scalars=(core, is_root),
    )


def solution(mesh):
    row, col = mesh.shape["row"], mesh.shape["col"]
    fine = Mesh(mesh.devices.reshape(8, 4, row // 32, col), ROW + ("col",))
    return jax.shard_map(
        on_device,
        mesh=fine,
        in_specs=(P(ROW, "col"), P(ROW, "col"), P(ROW), P(ROW, None), P("col")),
        out_specs=(P(ROW, "col"), P(None, "col")),
        check_vma=False,
    )
```

```python
import math

import jax
import jax.numpy as jnp
from jax import lax
from jax.experimental import pallas as pl
from jax.experimental.pallas import tpu as pltpu
from jax.sharding import Mesh, PartitionSpec as P

PANELS = 512
BLOCK = 128
SUB = 64
PIECES = 2
ROW = ("z", "x", "core")
VMEM = pl.BlockSpec(memory_space=pltpu.VMEM)
SMEM = pl.BlockSpec(memory_space=pltpu.SMEM)
HBM = pl.BlockSpec(memory_space=pltpu.MemorySpace.HBM)


def dot_fast(a, b, ca=1, cb=0):
    return lax.dot_general(
        a, b, (((ca,), (cb,)), ((), ())), preferred_element_type=jnp.float32
    )


def dot(a, b, ca=1, cb=0):
    return lax.dot_general(
        a,
        b,
        (((ca,), (cb,)), ((), ())),
        precision=lax.Precision.HIGHEST,
        preferred_element_type=jnp.float32,
    )


def split3(a):
    hi = a.astype(jnp.bfloat16)
    rest = a - hi.astype(jnp.float32)
    mid = rest.astype(jnp.bfloat16)
    low = (rest - mid.astype(jnp.float32)).astype(jnp.bfloat16)
    return hi, mid, low


def f32(*shape):
    return jax.ShapeDtypeStruct(shape, jnp.float32)


def call(
    kernel, out_shape, name, flops, *args, scalars=(), scratch=(), vmem=14, ins=None, outs=None
):
    return pl.pallas_call(
        kernel,
        out_shape=out_shape,
        in_specs=[SMEM] * len(scalars) + (ins or [VMEM] * len(args)),
        out_specs=outs or jax.tree.map(lambda _: VMEM, out_shape),
        scratch_shapes=scratch,
        name=name,
        compiler_params=pltpu.CompilerParams(vmem_limit_bytes=vmem << 20),
        cost_estimate=pl.CostEstimate(flops=flops, bytes_accessed=4 << 20, transcendentals=0),
    )(*[s.reshape(1, 1) for s in scalars], *args)


def iota(shape, axis):
    return lax.broadcasted_iota(jnp.int32, shape, axis)


def hot(mask):
    return mask.astype(jnp.float32).astype(jnp.bfloat16)


def eye(size):
    return (iota((size, size), 0) == iota((size, size), 1)).astype(jnp.float32)


def pack_kernel(height, capacity, child_hbm, rows_hbm, live_hbm, out_ref, rows_ref, live_ref, sems):
    count, width = child_hbm.shape
    copies = [
        pltpu.make_async_copy(live_hbm, live_ref, sems.at[0]),
        pltpu.make_async_copy(rows_hbm, rows_ref, sems.at[1]),
        pltpu.make_async_copy(child_hbm, out_ref.at[:, pl.ds(0, width)], sems.at[2]),
    ]
    for copy in copies:
        copy.start()
    copies[0].wait()
    copies[1].wait()
    owners = live_ref.shape[1]
    lanes = rows_ref.shape[1]
    live = jnp.broadcast_to(live_ref[...].astype(jnp.float32), (count, owners))
    owner = lax.div(iota((count, owners), 0), jnp.int32(capacity))
    live = jnp.sum(jnp.where(owner == iota((count, owners), 1), live, 0.0), axis=1, keepdims=True)
    slot = lax.rem(iota((count, 1), 0), jnp.int32(capacity)).astype(jnp.float32)
    local = lax.rem(rows_ref[...], jnp.int32(height)).astype(jnp.float32)
    identity = eye(lanes)
    rows = jnp.concatenate(
        [
            jnp.sum(jnp.broadcast_to(local[g : g + 1, :], (lanes, lanes)) * identity, axis=1, keepdims=True)
            for g in range(count // lanes)
        ],
        axis=0,
    )
    targets = jnp.where(slot < live, rows, -1.0)
    out_ref[:, width:] = jnp.broadcast_to(targets, (count, BLOCK))
    copies[2].wait()


def placed(front, rows, targets, cols):
    height, width = front.shape
    count, child_width = rows.shape
    col_hot = hot(iota((width, child_width), 0) == cols)
    row_hot = hot(iota((count, height), 1) == targets)
    total = front
    for term in split3(rows):
        spread = dot_fast(term, col_hot, 1, 1).astype(jnp.bfloat16)
        total = total + dot_fast(row_hot, spread, 0, 0)
    return total


def choose_kernel(root_ref, own_ref, *refs):
    arrived, out_ref = refs[:-1], refs[-1]
    total = arrived[0][...]
    for ref in arrived[1:]:
        total = total + ref[...]
    out_ref[...] = jnp.where(root_ref[0, 0] == 1, own_ref[...], total)


def add_kernel(a_ref, b_ref, out_ref):
    out_ref[...] = a_ref[...] + b_ref[...]


def fold_kernel(x_ref, out_ref):
    terms = [x_ref[i] for i in range(x_ref.shape[0])]
    while len(terms) > 1:
        terms = [a + b for a, b in zip(terms[::2], terms[1::2])]
    for i in range(out_ref.shape[0]):
        out_ref[i] = terms[0]


def first_kernel(x_ref, out_ref):
    for i in range(out_ref.shape[0]):
        out_ref[i] = x_ref[0]


def halves(core_ref, whole_ref, keep_ref, send_ref):
    height = keep_ref.shape[0]
    core = core_ref[0, 0]
    keep_ref[...] = whole_ref[pl.ds(pl.multiple_of(core * height, height), height), :]
    send_ref[...] = whole_ref[pl.ds(pl.multiple_of((1 - core) * height, height), height), :]


def gram_place(i, j):
    if i < 2:
        return (2 * j + i) * BLOCK
    return (2 * PANELS // BLOCK + 2 * (j - 2) + i - 2) * BLOCK


def place_kernel(
    core_ref, front_ref, arrived_ref, cols_ref, out_ref, keep_ref, send_ref, *refs
):
    share_refs, (whole_ref, copied_ref, sem) = refs[:-3], refs[-3:]
    child_width = cols_ref.shape[1]
    targets = arrived_ref[:, child_width : child_width + 1].astype(jnp.int32)
    front = placed(front_ref[...], arrived_ref[:, :child_width], targets, cols_ref[...])
    copied_ref[...] = front
    copy = pltpu.make_async_copy(copied_ref, out_ref, sem)
    copy.start()
    height = share_refs[0].shape[0]
    for k, ref in enumerate(share_refs):
        ref[...] = front[k * height : (k + 1) * height, :]
    half = PANELS // 2
    for first in range(2):
        cols = slice(half * first, PANELS)
        product = dot(front[:, half * first : half * (first + 1)], front[:, cols], 0, 0)
        for i in range(2):
            for j in range(2 * first, PANELS // BLOCK):
                at = gram_place(2 * first + i, j)
                left = (j - 2 * first) * BLOCK
                whole_ref[at : at + BLOCK, :] = product[i * BLOCK : (i + 1) * BLOCK, left : left + BLOCK]
    halves(core_ref, whole_ref, keep_ref, send_ref)
    copy.wait()


def product_kernel(core_ref, col_ref, front_ref, *refs):
    shares, (panel_ref, keep_ref, send_ref, whole_ref) = refs[:-4], refs[-4:]
    height, parts = shares[0].shape[0], len(shares)
    for k, ref in enumerate(shares):
        source = lax.rem(col_ref[0, 0] + (parts - k), jnp.int32(parts))
        panel_ref[pl.ds(pl.multiple_of(source * height, height), height), :] = ref[...]
    whole_ref[...] = dot(panel_ref[...], front_ref[...], 0, 0)
    halves(core_ref, whole_ref, keep_ref, send_ref)


def factor_diagonal(block):
    width = block.shape[1]
    done = []
    rest = block
    at_narrow, at_wide = iota((8, BLOCK), 0), iota((8, width), 0)
    count = SUB // 8
    for sub in range(BLOCK // SUB):
        groups = [rest[8 * g : 8 * g + 8, :] for g in range(count)]
        for p in range(count):
            first = SUB * sub + 8 * p
            spread = {
                (g, k): jnp.broadcast_to(groups[g][:, first + k : first + k + 1], (8, BLOCK))
                for g in range(p, count)
                for k in range(8)
            }
            for j in range(8):
                scale = lax.rsqrt(jnp.broadcast_to(spread[p, j][j : j + 1, :], (8, BLOCK)))
                factor = {g: spread[g, j] * scale for g in range(p, count)}
                factor[p] = jnp.where(at_narrow > j, factor[p], 0.0)
                for k in range(j + 1, 8):
                    pivot = jnp.broadcast_to(spread[p, k][j : j + 1, :], (8, BLOCK)) * scale
                    for g in range(p, count):
                        spread[g, k] = spread[g, k] - factor[g] * pivot
                wide = jnp.concatenate([scale] * (width // BLOCK), axis=1)
                row = jnp.broadcast_to(groups[p][j : j + 1, :], (8, width)) * wide
                for g in range(p, count):
                    updated = groups[g] - jnp.concatenate([factor[g]] * (width // BLOCK), axis=1) * row
                    groups[g] = jnp.where(at_wide == j, row, updated) if g == p else updated
        rows = jnp.concatenate(groups, axis=0)
        done.append(rows)
        if sub + 1 < BLOCK // SUB:
            rest = rest[SUB:, :] - dot(rows[:, SUB * (sub + 1) : BLOCK], rows, 0, 0)
    return jnp.concatenate(done, axis=0)


def in_order(core_ref, own, other):
    first = core_ref[0, 0] == 0
    return jnp.concatenate(
        [jnp.where(first, own, other), jnp.where(first, other, own)], axis=0
    )


def factor_kernel(piece, core_ref, own_ref, other_ref, *refs):
    above, out_ref = refs[:-1], refs[-1]
    n = PANELS
    per = n // BLOCK // PIECES
    gram = in_order(core_ref, own_ref[...], other_ref[...])
    identity = eye(BLOCK)

    def rows_of(block):
        at = block % per * BLOCK
        start = block // per * per * BLOCK
        return (*above, out_ref)[block // per], slice(at, at + BLOCK), start

    for k in range(piece * per, (piece + 1) * per):
        _, rows, start = rows_of(k)
        low, high = k * BLOCK, n + (k + 1) * BLOCK
        starts = [gram_place(k, j) for j in range(k, n // BLOCK)]
        pad = [jnp.zeros((BLOCK, low), jnp.float32)] if k else []
        work = jnp.concatenate([gram[at : at + BLOCK, :] for at in starts] + pad + [identity], axis=1)
        for upper in range(k):
            ref, at, shift = rows_of(upper)
            end = min(high, shift + ref.shape[1])
            factor = dot(ref[at, low - shift : low - shift + BLOCK], ref[at, low - shift : end - shift], 0, 0)
            if end < high:
                factor = jnp.concatenate([factor, jnp.zeros((BLOCK, high - end), jnp.float32)], axis=1)
            work = work - factor
        diagonal = factor_diagonal(jnp.concatenate([work[:, :BLOCK], identity], axis=1))
        out_ref[rows, low - start : high - start] = dot(diagonal[:, BLOCK:], work)
        out_ref[rows, low - start : low - start + BLOCK] = diagonal[:, :BLOCK]
        if low > start:
            out_ref[rows, : low - start] = jnp.zeros((BLOCK, low - start), jnp.float32)
        if high - start < out_ref.shape[1]:
            out_ref[rows, high - start :] = jnp.zeros((BLOCK, out_ref.shape[1] - high + start), jnp.float32)


def inverse_rows(blocks, i):
    per = blocks[0].shape[0]
    ref, at = blocks[i * BLOCK // per], i * BLOCK % per
    left = PANELS - i * BLOCK // per * per
    return ref[at : at + BLOCK, left : left + (i + 1) * BLOCK]


def last_factor_kernel(core_ref, own_ref, other_ref, panel_ref, *refs):
    blocks, basis_ref = refs[:-1], refs[-1]
    factor_kernel(PIECES - 1, core_ref, own_ref, other_ref, *blocks)
    for i in range(PANELS // BLOCK):
        upto = (i + 1) * BLOCK
        basis_ref[:, i * BLOCK : upto] = dot(panel_ref[:, :upto], inverse_rows(blocks, i), 1, 1)


def final_kernel(root_rows, core_ref, root_ref, *refs):
    ins, (out_hbm, factor_hbm), refs = refs[:6], refs[6:8], refs[8:]
    held, (out_ref, factor_ref, sems) = refs[:6], refs[6:]
    copies = [
        pltpu.make_async_copy(source, target, sems.at[i])
        for i, (source, target) in enumerate(zip(ins, held))
    ]
    for copy in copies:
        copy.start()
    upper_ref, lower_ref, own_ref, other_ref, basis_ref, front_ref = held
    blocks = (upper_ref, lower_ref)
    for copy in copies[:4]:
        copy.wait()
    sums = in_order(core_ref, own_ref[...], other_ref[...])
    coupled = jnp.concatenate(
        [dot(inverse_rows(blocks, i), sums[: (i + 1) * BLOCK, :]) for i in range(PANELS // BLOCK)],
        axis=0,
    )
    is_root = root_ref[0, 0] == 1
    per = PANELS // PIECES
    upper = jnp.concatenate(
        [
            jnp.concatenate(
                ([jnp.zeros((per, at), jnp.float32)] if at else []) + [ref[:, : PANELS - at]], axis=1
            )
            for ref, at in zip(blocks, range(0, PANELS, per))
        ],
        axis=0,
    )
    factor_ref[...] = jnp.where(is_root, upper, coupled) * (1.0 / root_rows)
    written = [pltpu.make_async_copy(factor_ref, factor_hbm, sems.at[6])]
    written[0].start()
    coupled_hi, coupled_mid, _ = split3(coupled)
    for copy in copies[4:]:
        copy.wait()
    half = out_ref.shape[0] // 2
    for i in range(2):
        rows = pl.ds(i * half, half)
        basis = basis_ref[rows, :]
        basis_hi, basis_mid, _ = split3(basis)
        update = dot_fast(basis_mid, coupled_hi) + dot_fast(basis_hi, coupled_mid)
        update = update + dot_fast(basis_hi, coupled_hi)
        out_ref[rows, :] = jnp.where(is_root, basis * root_rows, front_ref[rows, :] - update)
        written.append(
            pltpu.make_async_copy(out_ref.at[rows, :], out_hbm.at[rows, :], sems.at[7 + i])
        )
        written[-1].start()
    for copy in written:
        copy.wait()


def exchange(blocks, axis):
    return lax.all_to_all(blocks, axis, split_axis=0, concat_axis=0, tiled=True)


def swapped(x):
    return lax.ppermute(x, "core", [(0, 1), (1, 0)])


def summed(a, b):
    return call(add_kernel, f32(*a.shape), "add", 1 << 20, a, b, vmem=4)


def split_rows(x, n):
    return x.reshape(n, x.shape[0] // n, x.shape[1])


def merge_rows(x):
    return x.reshape(x.shape[0] * x.shape[1], x.shape[2])


def folded(x, n):
    return call(fold_kernel, f32(n, *x.shape[1:]), "fold", 1 << 20, x, vmem=6)


def on_device(front_in, child_block, child_rows, live_counts, column_map):
    rows_dev, cols_dev = front_in.shape
    owners, parts = lax.axis_size(ROW), lax.axis_size("col")
    chips = lax.axis_size(("z", "x"))
    count, child_width = child_block.shape
    capacity = count // owners
    core = lax.axis_index("core").astype(jnp.int32)
    col = lax.axis_index("col").astype(jnp.int32)
    is_root = (col == 0).astype(jnp.int32)
    halved = (f32(3 * PANELS // 2, BLOCK),) * 2
    local_cols = column_map % cols_dev

    sent = call(
        lambda *refs: pack_kernel(rows_dev, capacity, *refs),
        f32(count, child_width + BLOCK), "pack", 1 << 20,
        child_block, child_rows.reshape(count // BLOCK, BLOCK), live_counts,
        ins=[HBM] * 3,
        vmem=56,
        scratch=[
            pltpu.VMEM((count // BLOCK, BLOCK), jnp.int32),
            pltpu.VMEM((1, owners), jnp.int32),
            pltpu.SemaphoreType.DMA((3,)),
        ],
    )
    arrived = merge_rows(exchange(sent.reshape(owners, capacity, child_width + BLOCK), ROW))

    share = f32(rows_dev // parts, cols_dev)
    front, keep, send, *shares = call(
        place_kernel, [f32(rows_dev, cols_dev), *halved] + [share] * parts,
        "place", 4 << 30, front_in, arrived, local_cols.reshape(1, child_width), scalars=(core,),
        scratch=[
            pltpu.VMEM((3 * PANELS, BLOCK), jnp.float32),
            pltpu.VMEM((rows_dev, cols_dev), jnp.float32),
            pltpu.SemaphoreType.DMA,
        ],
        outs=[HBM] + [VMEM] * (parts + 2),
    )
    half = summed(keep, swapped(send))
    half, shares = lax.optimization_barrier((half, shares))
    sent_shares = [lax.ppermute(shares[k], "col", [(0, k)]) for k in range(1, parts)]
    panel_share = call(
        choose_kernel, share, "choose", 1 << 20, shares[0], *sent_shares, scalars=(is_root,), vmem=4
    )
    grams = exchange(split_rows(half, chips), ("z", "x"))
    grams, panel_share = lax.optimization_barrier((grams, panel_share))
    panel_shares = [panel_share] + [
        lax.ppermute(panel_share, "col", [(i, (i + k) % parts) for i in range(parts)])
        for k in range(1, parts)
    ]

    gram_share = exchange(folded(grams, parts), "col")
    gram_share, panel_shares[5:] = lax.optimization_barrier((gram_share, panel_shares[5:]))
    gram_share = call(
        first_kernel, f32(chips, *gram_share.shape[1:]), "first", 1 << 20, gram_share, vmem=4
    )
    own_gram = merge_rows(exchange(gram_share, ("z", "x")))
    other_gram = swapped(own_gram)

    panel, keep, send = call(
        product_kernel, (f32(rows_dev, PANELS),) + (f32(PANELS // 2, cols_dev),) * 2,
        "products", 2 << 30, front, *panel_shares, scalars=(core, col), scratch=[pltpu.VMEM((PANELS, cols_dev), jnp.float32)],
    )
    half = summed(keep, swapped(send))
    summands = exchange(split_rows(half, chips), ("z", "x"))

    block_shape = f32(PANELS // PIECES, 3 * PANELS // 2)
    upper = call(
        lambda *refs: factor_kernel(0, *refs), block_shape, "factor0", 10 << 30,
        own_gram, other_gram, scalars=(core,),
    )
    summands, upper = lax.optimization_barrier((summands, upper))
    own_sums = merge_rows(exchange(folded(summands, chips), ("z", "x")))
    lower, basis = call(
        last_factor_kernel, (block_shape, f32(rows_dev, PANELS)), "factor1", 12 << 30,
        own_gram, other_gram, panel, upper, scalars=(core,),
    )
    own_sums, basis = lax.optimization_barrier((own_sums, basis))
    other_sums = swapped(own_sums)
    whole = (rows_dev, cols_dev)
    ins = (upper, lower, own_sums, other_sums, basis, front)
    return call(
        lambda *refs: final_kernel(math.sqrt(rows_dev * owners), *refs),
        (f32(*whole), f32(PANELS, cols_dev)), "final", 4 << 30, *ins, scalars=(core, is_root),
        ins=[HBM] * len(ins), outs=(HBM, HBM), vmem=56,
        scratch=[pltpu.VMEM(x.shape, jnp.float32) for x in ins]
        + [pltpu.VMEM(whole, jnp.float32), pltpu.VMEM((PANELS, cols_dev), jnp.float32)]
        + [pltpu.SemaphoreType.DMA((9,))],
    )


def solution(mesh):
    row, col = mesh.shape["row"], mesh.shape["col"]
    fine = Mesh(mesh.devices.reshape(8, 4, row // 32, col), ROW + ("col",))
    return jax.shard_map(
        on_device,
        mesh=fine,
        in_specs=(P(ROW, "col"), P(ROW, "col"), P(ROW), P(ROW, None), P("col")),
        out_specs=(P(ROW, "col"), P(None, "col")),
        check_vma=False,
    )
```

```python
import math

import jax
import jax.numpy as jnp
from jax import lax
from jax.experimental import pallas as pl
from jax.experimental.pallas import tpu as pltpu
from jax.sharding import Mesh, PartitionSpec as P

PANELS = 512
BLOCK = 128
SUB = 64
PIECES = 2
ROW = ("z", "x", "core")
VMEM = pl.BlockSpec(memory_space=pltpu.VMEM)
SMEM = pl.BlockSpec(memory_space=pltpu.SMEM)
HBM = pl.BlockSpec(memory_space=pltpu.MemorySpace.HBM)


def dot_fast(a, b, ca=1, cb=0):
    return lax.dot_general(
        a, b, (((ca,), (cb,)), ((), ())), preferred_element_type=jnp.float32
    )


def dot(a, b, ca=1, cb=0):
    return lax.dot_general(
        a,
        b,
        (((ca,), (cb,)), ((), ())),
        precision=lax.Precision.HIGHEST,
        preferred_element_type=jnp.float32,
    )


def split3(a):
    hi = a.astype(jnp.bfloat16)
    rest = a - hi.astype(jnp.float32)
    mid = rest.astype(jnp.bfloat16)
    low = (rest - mid.astype(jnp.float32)).astype(jnp.bfloat16)
    return hi, mid, low


def f32(*shape):
    return jax.ShapeDtypeStruct(shape, jnp.float32)


def call(
    kernel, out_shape, name, flops, *args, scalars=(), scratch=(), vmem=14, ins=None, outs=None
):
    return pl.pallas_call(
        kernel,
        out_shape=out_shape,
        in_specs=[SMEM] * len(scalars) + (ins or [VMEM] * len(args)),
        out_specs=outs or jax.tree.map(lambda _: VMEM, out_shape),
        scratch_shapes=scratch,
        name=name,
        compiler_params=pltpu.CompilerParams(vmem_limit_bytes=vmem << 20),
        cost_estimate=pl.CostEstimate(flops=flops, bytes_accessed=4 << 20, transcendentals=0),
    )(*[s.reshape(1, 1) for s in scalars], *args)


def iota(shape, axis):
    return lax.broadcasted_iota(jnp.int32, shape, axis)


def hot(mask):
    return mask.astype(jnp.float32).astype(jnp.bfloat16)


def eye(size):
    return (iota((size, size), 0) == iota((size, size), 1)).astype(jnp.float32)


def pack_kernel(height, capacity, child_hbm, rows_hbm, live_hbm, out_ref, rows_ref, live_ref, sems):
    count, width = child_hbm.shape
    copies = [
        pltpu.make_async_copy(live_hbm, live_ref, sems.at[0]),
        pltpu.make_async_copy(rows_hbm, rows_ref, sems.at[1]),
        pltpu.make_async_copy(child_hbm, out_ref.at[:, pl.ds(0, width)], sems.at[2]),
    ]
    for copy in copies:
        copy.start()
    copies[0].wait()
    copies[1].wait()
    owners = live_ref.shape[1]
    lanes = rows_ref.shape[1]
    live = jnp.broadcast_to(live_ref[...].astype(jnp.float32), (count, owners))
    owner = lax.div(iota((count, owners), 0), jnp.int32(capacity))
    live = jnp.sum(jnp.where(owner == iota((count, owners), 1), live, 0.0), axis=1, keepdims=True)
    slot = lax.rem(iota((count, 1), 0), jnp.int32(capacity)).astype(jnp.float32)
    local = lax.rem(rows_ref[...], jnp.int32(height)).astype(jnp.float32)
    identity = eye(lanes)
    rows = jnp.concatenate(
        [
            jnp.sum(jnp.broadcast_to(local[g : g + 1, :], (lanes, lanes)) * identity, axis=1, keepdims=True)
            for g in range(count // lanes)
        ],
        axis=0,
    )
    targets = jnp.where(slot < live, rows, -1.0)
    out_ref[:, width:] = jnp.broadcast_to(targets, (count, BLOCK))
    copies[2].wait()


def placed(front, rows, targets, cols):
    height, width = front.shape
    count, child_width = rows.shape
    col_hot = hot(iota((width, child_width), 0) == cols)
    row_hot = hot(iota((count, height), 1) == targets)
    total = front
    for term in split3(rows):
        spread = dot_fast(term, col_hot, 1, 1).astype(jnp.bfloat16)
        total = total + dot_fast(row_hot, spread, 0, 0)
    return total


def bundle_kernel(root_ref, grams_ref, own_ref, *refs):
    arrived, out_ref = refs[:-1], refs[-1]
    share = total([ref[...] for ref in arrived])
    share = jnp.where(root_ref[0, 0] == 1, own_ref[...], share)
    gram = total([grams_ref[i] for i in range(grams_ref.shape[0])])
    height = share.shape[0]
    for i in range(out_ref.shape[0]):
        for lanes in range(share.shape[1] // BLOCK):
            out_ref[i, lanes * height : (lanes + 1) * height, :] = share[
                :, lanes * BLOCK : (lanes + 1) * BLOCK
            ]
        out_ref[i, share.shape[1] // BLOCK * height :, :] = gram


def total(terms):
    while len(terms) > 1:
        pairs = [a + b for a, b in zip(terms[::2], terms[1::2])]
        terms = pairs + terms[len(pairs) * 2 :]
    return terms[0]


def add_kernel(a_ref, b_ref, out_ref):
    out_ref[...] = a_ref[...] + b_ref[...]


def fold_kernel(x_ref, out_ref):
    x = total([x_ref[i] for i in range(x_ref.shape[0])])
    for i in range(out_ref.shape[0]):
        out_ref[i] = x


def gram_kernel(bundle_ref, out_ref):
    height = out_ref.shape[1]
    for i in range(out_ref.shape[0]):
        out_ref[i] = bundle_ref[0, bundle_ref.shape[1] - height :, :]


def halves(core_ref, whole_ref, keep_ref, send_ref):
    height = keep_ref.shape[0]
    core = core_ref[0, 0]
    keep_ref[...] = whole_ref[pl.ds(pl.multiple_of(core * height, height), height), :]
    send_ref[...] = whole_ref[pl.ds(pl.multiple_of((1 - core) * height, height), height), :]


def gram_place(i, j):
    if i < 2:
        return (2 * j + i) * BLOCK
    return (2 * PANELS // BLOCK + 2 * (j - 2) + i - 2) * BLOCK


def place_kernel(
    core_ref, front_ref, arrived_ref, cols_ref, out_ref, keep_ref, send_ref, *refs
):
    share_refs, whole_ref = refs[:-1], refs[-1]
    child_width = cols_ref.shape[1]
    targets = arrived_ref[:, child_width : child_width + 1].astype(jnp.int32)
    front = placed(front_ref[...], arrived_ref[:, :child_width], targets, cols_ref[...])
    out_ref[...] = front
    height = share_refs[0].shape[0]
    for k, ref in enumerate(share_refs):
        ref[...] = front[k * height : (k + 1) * height, :]
    half = PANELS // 2
    for first in range(2):
        cols = slice(half * first, PANELS)
        product = dot(front[:, half * first : half * (first + 1)], front[:, cols], 0, 0)
        for i in range(2):
            for j in range(2 * first, PANELS // BLOCK):
                at = gram_place(2 * first + i, j)
                left = (j - 2 * first) * BLOCK
                whole_ref[at : at + BLOCK, :] = product[i * BLOCK : (i + 1) * BLOCK, left : left + BLOCK]
    halves(core_ref, whole_ref, keep_ref, send_ref)


def product_kernel(core_ref, front_ref, bundle_ref, panel_ref, keep_ref, send_ref, whole_ref):
    parts = bundle_ref.shape[0]
    height = panel_ref.shape[0] // parts
    for k in range(parts):
        for lanes in range(panel_ref.shape[1] // BLOCK):
            panel_ref[k * height : (k + 1) * height, lanes * BLOCK : (lanes + 1) * BLOCK] = bundle_ref[
                k, lanes * height : (lanes + 1) * height, :
            ]
    whole_ref[...] = dot(panel_ref[...], front_ref[...], 0, 0)
    halves(core_ref, whole_ref, keep_ref, send_ref)


def factor_diagonal(block):
    width = block.shape[1]
    done = []
    rest = block
    at_narrow, at_wide = iota((8, BLOCK), 0), iota((8, width), 0)
    count = SUB // 8
    for sub in range(BLOCK // SUB):
        groups = [rest[8 * g : 8 * g + 8, :] for g in range(count)]
        for p in range(count):
            first = SUB * sub + 8 * p
            spread = {
                (g, k): jnp.broadcast_to(groups[g][:, first + k : first + k + 1], (8, BLOCK))
                for g in range(p, count)
                for k in range(8)
            }
            for j in range(8):
                scale = lax.rsqrt(jnp.broadcast_to(spread[p, j][j : j + 1, :], (8, BLOCK)))
                factor = {g: spread[g, j] * scale for g in range(p, count)}
                factor[p] = jnp.where(at_narrow > j, factor[p], 0.0)
                for k in range(j + 1, 8):
                    pivot = jnp.broadcast_to(spread[p, k][j : j + 1, :], (8, BLOCK)) * scale
                    for g in range(p, count):
                        spread[g, k] = spread[g, k] - factor[g] * pivot
                wide = jnp.concatenate([scale] * (width // BLOCK), axis=1)
                row = jnp.broadcast_to(groups[p][j : j + 1, :], (8, width)) * wide
                for g in range(p, count):
                    updated = groups[g] - jnp.concatenate([factor[g]] * (width // BLOCK), axis=1) * row
                    groups[g] = jnp.where(at_wide == j, row, updated) if g == p else updated
        rows = jnp.concatenate(groups, axis=0)
        done.append(rows)
        if sub + 1 < BLOCK // SUB:
            rest = rest[SUB:, :] - dot(rows[:, SUB * (sub + 1) : BLOCK], rows, 0, 0)
    return jnp.concatenate(done, axis=0)


def in_order(core_ref, own, other):
    first = core_ref[0, 0] == 0
    return jnp.concatenate(
        [jnp.where(first, own, other), jnp.where(first, other, own)], axis=0
    )


def factor_kernel(piece, core_ref, own_ref, other_ref, *refs):
    above, out_ref = refs[:-1], refs[-1]
    n = PANELS
    per = n // BLOCK // PIECES
    gram = in_order(core_ref, own_ref[...], other_ref[...])
    identity = eye(BLOCK)

    def rows_of(block):
        at = block % per * BLOCK
        start = block // per * per * BLOCK
        return (*above, out_ref)[block // per], slice(at, at + BLOCK), start

    for k in range(piece * per, (piece + 1) * per):
        _, rows, start = rows_of(k)
        low, high = k * BLOCK, n + (k + 1) * BLOCK
        starts = [gram_place(k, j) for j in range(k, n // BLOCK)]
        pad = [jnp.zeros((BLOCK, low), jnp.float32)] if k else []
        work = jnp.concatenate([gram[at : at + BLOCK, :] for at in starts] + pad + [identity], axis=1)
        for upper in range(k):
            ref, at, shift = rows_of(upper)
            end = min(high, shift + ref.shape[1])
            factor = dot(ref[at, low - shift : low - shift + BLOCK], ref[at, low - shift : end - shift], 0, 0)
            if end < high:
                factor = jnp.concatenate([factor, jnp.zeros((BLOCK, high - end), jnp.float32)], axis=1)
            work = work - factor
        diagonal = factor_diagonal(jnp.concatenate([work[:, :BLOCK], identity], axis=1))
        out_ref[rows, low - start : high - start] = dot(diagonal[:, BLOCK:], work)
        out_ref[rows, low - start : low - start + BLOCK] = diagonal[:, :BLOCK]
        if low > start:
            out_ref[rows, : low - start] = jnp.zeros((BLOCK, low - start), jnp.float32)
        if high - start < out_ref.shape[1]:
            out_ref[rows, high - start :] = jnp.zeros((BLOCK, out_ref.shape[1] - high + start), jnp.float32)


def inverse_rows(blocks, i):
    per = blocks[0].shape[0]
    ref, at = blocks[i * BLOCK // per], i * BLOCK % per
    left = PANELS - i * BLOCK // per * per
    return ref[at : at + BLOCK, left : left + (i + 1) * BLOCK]


def last_factor_kernel(core_ref, own_ref, other_ref, panel_ref, *refs):
    blocks, basis_ref = refs[:-1], refs[-1]
    factor_kernel(PIECES - 1, core_ref, own_ref, other_ref, *blocks)
    for i in range(PANELS // BLOCK):
        upto = (i + 1) * BLOCK
        basis_ref[:, i * BLOCK : upto] = dot(panel_ref[:, :upto], inverse_rows(blocks, i), 1, 1)


def final_kernel(root_rows, core_ref, root_ref, *refs):
    ins, (out_hbm, factor_hbm), refs = refs[:6], refs[6:8], refs[8:]
    held, (out_ref, factor_ref, sems) = refs[:6], refs[6:]
    copies = [
        pltpu.make_async_copy(source, target, sems.at[i])
        for i, (source, target) in enumerate(zip(ins, held))
    ]
    for copy in copies:
        copy.start()
    upper_ref, lower_ref, own_ref, other_ref, basis_ref, front_ref = held
    blocks = (upper_ref, lower_ref)
    for copy in copies[:4]:
        copy.wait()
    sums = in_order(core_ref, own_ref[...], other_ref[...])
    coupled = jnp.concatenate(
        [dot(inverse_rows(blocks, i), sums[: (i + 1) * BLOCK, :]) for i in range(PANELS // BLOCK)],
        axis=0,
    )
    is_root = root_ref[0, 0] == 1
    per = PANELS // PIECES
    upper = jnp.concatenate(
        [
            jnp.concatenate(
                ([jnp.zeros((per, at), jnp.float32)] if at else []) + [ref[:, : PANELS - at]], axis=1
            )
            for ref, at in zip(blocks, range(0, PANELS, per))
        ],
        axis=0,
    )
    factor_ref[...] = jnp.where(is_root, upper, coupled) * (1.0 / root_rows)
    written = [pltpu.make_async_copy(factor_ref, factor_hbm, sems.at[6])]
    written[0].start()
    coupled_hi, coupled_mid, _ = split3(coupled)
    for copy in copies[4:]:
        copy.wait()
    half = out_ref.shape[0] // 2
    for i in range(2):
        rows = pl.ds(i * half, half)
        basis = basis_ref[rows, :]
        basis_hi, basis_mid, _ = split3(basis)
        update = dot_fast(basis_mid, coupled_hi) + dot_fast(basis_hi, coupled_mid)
        update = update + dot_fast(basis_hi, coupled_hi)
        out_ref[rows, :] = jnp.where(is_root, basis * root_rows, front_ref[rows, :] - update)
        written.append(
            pltpu.make_async_copy(out_ref.at[rows, :], out_hbm.at[rows, :], sems.at[7 + i])
        )
        written[-1].start()
    for copy in written:
        copy.wait()


def exchange(blocks, axis):
    return lax.all_to_all(blocks, axis, split_axis=0, concat_axis=0, tiled=True)


def swapped(x):
    return lax.ppermute(x, "core", [(0, 1), (1, 0)])


def summed(a, b):
    return call(add_kernel, f32(*a.shape), "add", 1 << 20, a, b, vmem=4)


def split_rows(x, n):
    return x.reshape(n, x.shape[0] // n, x.shape[1])


def merge_rows(x):
    return x.reshape(x.shape[0] * x.shape[1], x.shape[2])


def folded(x, n):
    return call(fold_kernel, f32(n, *x.shape[1:]), "fold", 1 << 20, x, vmem=6)


def on_device(front_in, child_block, child_rows, live_counts, column_map):
    rows_dev, cols_dev = front_in.shape
    owners, parts = lax.axis_size(ROW), lax.axis_size("col")
    chips = lax.axis_size(("z", "x"))
    count, child_width = child_block.shape
    capacity = count // owners
    core = lax.axis_index("core").astype(jnp.int32)
    col = lax.axis_index("col").astype(jnp.int32)
    is_root = (col == 0).astype(jnp.int32)
    halved = (f32(3 * PANELS // 2, BLOCK),) * 2
    local_cols = column_map % cols_dev

    sent = call(
        lambda *refs: pack_kernel(rows_dev, capacity, *refs),
        f32(count, child_width + BLOCK), "pack", 1 << 20,
        child_block, child_rows.reshape(count // BLOCK, BLOCK), live_counts,
        ins=[HBM] * 3,
        vmem=56,
        scratch=[
            pltpu.VMEM((count // BLOCK, BLOCK), jnp.int32),
            pltpu.VMEM((1, owners), jnp.int32),
            pltpu.SemaphoreType.DMA((3,)),
        ],
    )
    arrived = merge_rows(exchange(sent.reshape(owners, capacity, child_width + BLOCK), ROW))

    share = f32(rows_dev // parts, cols_dev)
    front, keep, send, *shares = call(
        place_kernel, [f32(rows_dev, cols_dev), *halved] + [share] * parts,
        "place", 4 << 30, front_in, arrived, local_cols.reshape(1, child_width), scalars=(core,),
        scratch=[pltpu.VMEM((3 * PANELS, BLOCK), jnp.float32)],
    )
    half = summed(keep, swapped(send))
    half, shares = lax.optimization_barrier((half, shares))
    sent_shares = [lax.ppermute(shares[k], "col", [(0, k)]) for k in range(1, parts)]
    grams = exchange(split_rows(half, chips), ("z", "x"))
    share_rows = rows_dev // parts * PANELS // BLOCK
    gram_rows = grams.shape[1]
    bundle = call(
        bundle_kernel, f32(parts, share_rows + gram_rows, BLOCK), "bundle", 1 << 20,
        grams, shares[0], *sent_shares, scalars=(is_root,), vmem=8,
    )
    bundle = exchange(bundle, "col")
    gram_share = call(
        gram_kernel, f32(chips, gram_rows, BLOCK), "gram_share", 1 << 20, bundle, vmem=6
    )
    own_gram = merge_rows(exchange(gram_share, ("z", "x")))
    other_gram = swapped(own_gram)

    panel, keep, send = call(
        product_kernel, (f32(rows_dev, PANELS),) + (f32(PANELS // 2, cols_dev),) * 2,
        "products", 2 << 30, front, bundle, scalars=(core,),
        scratch=[pltpu.VMEM((PANELS, cols_dev), jnp.float32)],
    )
    half = summed(keep, swapped(send))
    summands = exchange(split_rows(half, chips), ("z", "x"))

    block_shape = f32(PANELS // PIECES, 3 * PANELS // 2)
    upper = call(
        lambda *refs: factor_kernel(0, *refs), block_shape, "factor0", 10 << 30,
        own_gram, other_gram, scalars=(core,),
    )
    summands, upper = lax.optimization_barrier((summands, upper))
    own_sums = merge_rows(exchange(folded(summands, chips), ("z", "x")))
    lower, basis = call(
        last_factor_kernel, (block_shape, f32(rows_dev, PANELS)), "factor1", 12 << 30,
        own_gram, other_gram, panel, upper, scalars=(core,),
    )
    own_sums, basis = lax.optimization_barrier((own_sums, basis))
    other_sums = swapped(own_sums)
    whole = (rows_dev, cols_dev)
    ins = (upper, lower, own_sums, other_sums, basis, front)
    return call(
        lambda *refs: final_kernel(math.sqrt(rows_dev * owners), *refs),
        (f32(*whole), f32(PANELS, cols_dev)), "final", 4 << 30, *ins, scalars=(core, is_root),
        ins=[HBM] * len(ins), outs=(HBM, HBM), vmem=56,
        scratch=[pltpu.VMEM(x.shape, jnp.float32) for x in ins]
        + [pltpu.VMEM(whole, jnp.float32), pltpu.VMEM((PANELS, cols_dev), jnp.float32)]
        + [pltpu.SemaphoreType.DMA((9,))],
    )


def solution(mesh):
    row, col = mesh.shape["row"], mesh.shape["col"]
    fine = Mesh(mesh.devices.reshape(8, 4, row // 32, col), ROW + ("col",))
    return jax.shard_map(
        on_device,
        mesh=fine,
        in_specs=(P(ROW, "col"), P(ROW, "col"), P(ROW), P(ROW, None), P("col")),
        out_specs=(P(ROW, "col"), P(None, "col")),
        check_vma=False,
    )
```

```python
import math

import jax
import jax.numpy as jnp
from jax import lax
from jax.experimental import pallas as pl
from jax.experimental.pallas import tpu as pltpu
from jax.sharding import Mesh, PartitionSpec as P

PANELS = 512
BLOCK = 128
SUB = 64
PIECES = 2
ROW = ("z", "x", "core")
VMEM = pl.BlockSpec(memory_space=pltpu.VMEM)
SMEM = pl.BlockSpec(memory_space=pltpu.SMEM)
HBM = pl.BlockSpec(memory_space=pltpu.MemorySpace.HBM)


def dot_fast(a, b, ca=1, cb=0):
    return lax.dot_general(
        a, b, (((ca,), (cb,)), ((), ())), preferred_element_type=jnp.float32
    )


def dot(a, b, ca=1, cb=0):
    return lax.dot_general(
        a,
        b,
        (((ca,), (cb,)), ((), ())),
        precision=lax.Precision.HIGHEST,
        preferred_element_type=jnp.float32,
    )


def split3(a):
    hi = a.astype(jnp.bfloat16)
    rest = a - hi.astype(jnp.float32)
    mid = rest.astype(jnp.bfloat16)
    low = (rest - mid.astype(jnp.float32)).astype(jnp.bfloat16)
    return hi, mid, low


def f32(*shape):
    return jax.ShapeDtypeStruct(shape, jnp.float32)


def call(
    kernel, out_shape, name, flops, *args, scalars=(), scratch=(), vmem=14, ins=None, outs=None
):
    return pl.pallas_call(
        kernel,
        out_shape=out_shape,
        in_specs=[SMEM] * len(scalars) + (ins or [VMEM] * len(args)),
        out_specs=outs or jax.tree.map(lambda _: VMEM, out_shape),
        scratch_shapes=scratch,
        name=name,
        compiler_params=pltpu.CompilerParams(vmem_limit_bytes=vmem << 20),
        cost_estimate=pl.CostEstimate(flops=flops, bytes_accessed=4 << 20, transcendentals=0),
    )(*[s.reshape(1, 1) for s in scalars], *args)


def iota(shape, axis):
    return lax.broadcasted_iota(jnp.int32, shape, axis)


def hot(mask):
    return mask.astype(jnp.float32).astype(jnp.bfloat16)


def eye(size):
    return (iota((size, size), 0) == iota((size, size), 1)).astype(jnp.float32)


def pack_kernel(height, child_hbm, rows_hbm, live_hbm, out_ref, child_ref, rows_ref, live_ref, sems):
    copies = [
        pltpu.make_async_copy(live_hbm, live_ref, sems.at[0]),
        pltpu.make_async_copy(rows_hbm, rows_ref, sems.at[1]),
        pltpu.make_async_copy(child_hbm, child_ref, sems.at[2]),
    ]
    for copy in copies:
        copy.start()
    copies[0].wait()
    copies[1].wait()
    count, width = child_ref.shape
    owners = live_ref.shape[1]
    capacity, lanes = count // owners, rows_ref.shape[1]
    live = jnp.broadcast_to(live_ref[...].astype(jnp.float32), (count, owners))
    owner = lax.div(iota((count, owners), 0), jnp.int32(capacity))
    live = jnp.sum(jnp.where(owner == iota((count, owners), 1), live, 0.0), axis=1, keepdims=True)
    slot = lax.rem(iota((count, 1), 0), jnp.int32(capacity))
    local = lax.rem(rows_ref[...], jnp.int32(height)).astype(jnp.float32)
    identity = eye(lanes)
    rows = jnp.concatenate(
        [
            jnp.sum(jnp.broadcast_to(local[g : g + 1, :], (lanes, lanes)) * identity, axis=1, keepdims=True)
            for g in range(count // lanes)
        ],
        axis=0,
    )
    places = jnp.where(slot.astype(jnp.float32) < live, rows, -1.0)
    spread = jnp.where(iota((count, lanes), 1) == slot, jnp.broadcast_to(places, (count, lanes)), 0.0)
    places = jnp.sum(spread.reshape(owners, capacity, lanes), axis=1)
    copies[2].wait()
    step = out_ref.shape[0] // owners
    for s in range(owners):
        for h in range(width // BLOCK):
            at = s * step + h * capacity
            out_ref[at : at + capacity, :] = child_ref[
                s * capacity : (s + 1) * capacity, h * BLOCK : (h + 1) * BLOCK
            ]
        out_ref[s * step + step - 1 : s * step + step, :] = places[s : s + 1, :]


def unpacked(ref, owners, capacity, width):
    step = ref.shape[0] // owners
    rows = jnp.concatenate(
        [
            jnp.concatenate(
                [
                    ref[s * step + h * capacity : s * step + (h + 1) * capacity, :]
                    for s in range(owners)
                ],
                axis=0,
            )
            for h in range(width // BLOCK)
        ],
        axis=1,
    )
    shape = (owners * capacity, BLOCK)
    places = jnp.concatenate(
        [
            jnp.broadcast_to(ref[s * step + step - 1 : s * step + step, :], (capacity, BLOCK))
            for s in range(owners)
        ],
        axis=0,
    )
    own = iota(shape, 1) == lax.rem(iota(shape, 0), jnp.int32(capacity))
    places = jnp.sum(jnp.where(own, places, 0.0), axis=1, keepdims=True)
    return rows, places.astype(jnp.int32)


def placed(front, rows, targets, cols):
    height, width = front.shape
    count, child_width = rows.shape
    col_hot = hot(iota((width, child_width), 0) == cols)
    row_hot = hot(iota((count, height), 1) == targets)
    total = front
    for term in split3(rows):
        spread = dot_fast(term, col_hot, 1, 1).astype(jnp.bfloat16)
        total = total + dot_fast(row_hot, spread, 0, 0)
    return total


def bundle_kernel(root_ref, grams_ref, own_ref, *refs):
    arrived, out_ref = refs[:-1], refs[-1]
    share = total([ref[...] for ref in arrived])
    share = jnp.where(root_ref[0, 0] == 1, own_ref[...], share)
    gram = total([grams_ref[i] for i in range(grams_ref.shape[0])])
    height = share.shape[0]
    for i in range(out_ref.shape[0]):
        for lanes in range(share.shape[1] // BLOCK):
            out_ref[i, lanes * height : (lanes + 1) * height, :] = share[
                :, lanes * BLOCK : (lanes + 1) * BLOCK
            ]
        out_ref[i, share.shape[1] // BLOCK * height :, :] = gram


def total(terms):
    while len(terms) > 1:
        pairs = [a + b for a, b in zip(terms[::2], terms[1::2])]
        terms = pairs + terms[len(pairs) * 2 :]
    return terms[0]


def add_kernel(a_ref, b_ref, out_ref):
    out_ref[...] = a_ref[...] + b_ref[...]


def fold_kernel(x_ref, out_ref):
    x = total([x_ref[i] for i in range(x_ref.shape[0])])
    for i in range(out_ref.shape[0]):
        out_ref[i] = x


def gram_kernel(bundle_ref, out_ref):
    height = out_ref.shape[1]
    for i in range(out_ref.shape[0]):
        out_ref[i] = bundle_ref[0, bundle_ref.shape[1] - height :, :]


def halves(core_ref, whole_ref, keep_ref, send_ref):
    height = keep_ref.shape[0]
    core = core_ref[0, 0]
    keep_ref[...] = whole_ref[pl.ds(pl.multiple_of(core * height, height), height), :]
    send_ref[...] = whole_ref[pl.ds(pl.multiple_of((1 - core) * height, height), height), :]


def gram_place(i, j):
    if i < 2:
        return (2 * j + i) * BLOCK
    return (2 * PANELS // BLOCK + 2 * (j - 2) + i - 2) * BLOCK


def place_kernel(
    owners, core_ref, front_ref, arrived_ref, cols_ref, out_ref, keep_ref, send_ref, *refs
):
    share_refs, whole_ref = refs[:-1], refs[-1]
    width = cols_ref.shape[1]
    capacity = (arrived_ref.shape[0] // owners - 1) // (width // BLOCK)
    rows, places = unpacked(arrived_ref, owners, capacity, width)
    front = placed(front_ref[...], rows, places, cols_ref[...])
    out_ref[...] = front
    height = share_refs[0].shape[0]
    for k, ref in enumerate(share_refs):
        ref[...] = front[k * height : (k + 1) * height, :]
    half = PANELS // 2
    for first in range(2):
        cols = slice(half * first, PANELS)
        product = dot(front[:, half * first : half * (first + 1)], front[:, cols], 0, 0)
        for i in range(2):
            for j in range(2 * first, PANELS // BLOCK):
                at = gram_place(2 * first + i, j)
                left = (j - 2 * first) * BLOCK
                whole_ref[at : at + BLOCK, :] = product[i * BLOCK : (i + 1) * BLOCK, left : left + BLOCK]
    halves(core_ref, whole_ref, keep_ref, send_ref)


def product_kernel(core_ref, front_ref, bundle_ref, panel_ref, keep_ref, send_ref, whole_ref):
    parts = bundle_ref.shape[0]
    height = panel_ref.shape[0] // parts
    for k in range(parts):
        for lanes in range(panel_ref.shape[1] // BLOCK):
            panel_ref[k * height : (k + 1) * height, lanes * BLOCK : (lanes + 1) * BLOCK] = bundle_ref[
                k, lanes * height : (lanes + 1) * height, :
            ]
    whole_ref[...] = dot(panel_ref[...], front_ref[...], 0, 0)
    halves(core_ref, whole_ref, keep_ref, send_ref)


def factor_diagonal(block):
    width = block.shape[1]
    done = []
    rest = block
    at_narrow, at_wide = iota((8, BLOCK), 0), iota((8, width), 0)
    count = SUB // 8
    for sub in range(BLOCK // SUB):
        groups = [rest[8 * g : 8 * g + 8, :] for g in range(count)]
        for p in range(count):
            first = SUB * sub + 8 * p
            spread = {
                (g, k): jnp.broadcast_to(groups[g][:, first + k : first + k + 1], (8, BLOCK))
                for g in range(p, count)
                for k in range(8)
            }
            for j in range(8):
                scale = lax.rsqrt(jnp.broadcast_to(spread[p, j][j : j + 1, :], (8, BLOCK)))
                factor = {g: spread[g, j] * scale for g in range(p, count)}
                factor[p] = jnp.where(at_narrow > j, factor[p], 0.0)
                for k in range(j + 1, 8):
                    pivot = jnp.broadcast_to(spread[p, k][j : j + 1, :], (8, BLOCK)) * scale
                    for g in range(p, count):
                        spread[g, k] = spread[g, k] - factor[g] * pivot
                wide = jnp.concatenate([scale] * (width // BLOCK), axis=1)
                row = jnp.broadcast_to(groups[p][j : j + 1, :], (8, width)) * wide
                for g in range(p, count):
                    updated = groups[g] - jnp.concatenate([factor[g]] * (width // BLOCK), axis=1) * row
                    groups[g] = jnp.where(at_wide == j, row, updated) if g == p else updated
        rows = jnp.concatenate(groups, axis=0)
        done.append(rows)
        if sub + 1 < BLOCK // SUB:
            rest = rest[SUB:, :] - dot(rows[:, SUB * (sub + 1) : BLOCK], rows, 0, 0)
    return jnp.concatenate(done, axis=0)


def in_order(core_ref, own, other):
    first = core_ref[0, 0] == 0
    return jnp.concatenate(
        [jnp.where(first, own, other), jnp.where(first, other, own)], axis=0
    )


def factor_kernel(piece, core_ref, own_ref, other_ref, *refs):
    above, out_ref = refs[:-1], refs[-1]
    n = PANELS
    per = n // BLOCK // PIECES
    gram = in_order(core_ref, own_ref[...], other_ref[...])
    identity = eye(BLOCK)

    def rows_of(block):
        at = block % per * BLOCK
        start = block // per * per * BLOCK
        return (*above, out_ref)[block // per], slice(at, at + BLOCK), start

    for k in range(piece * per, (piece + 1) * per):
        _, rows, start = rows_of(k)
        low, high = k * BLOCK, n + (k + 1) * BLOCK
        starts = [gram_place(k, j) for j in range(k, n // BLOCK)]
        pad = [jnp.zeros((BLOCK, low), jnp.float32)] if k else []
        work = jnp.concatenate([gram[at : at + BLOCK, :] for at in starts] + pad + [identity], axis=1)
        for upper in range(k):
            ref, at, shift = rows_of(upper)
            end = min(high, shift + ref.shape[1])
            factor = dot(ref[at, low - shift : low - shift + BLOCK], ref[at, low - shift : end - shift], 0, 0)
            if end < high:
                factor = jnp.concatenate([factor, jnp.zeros((BLOCK, high - end), jnp.float32)], axis=1)
            work = work - factor
        diagonal = factor_diagonal(jnp.concatenate([work[:, :BLOCK], identity], axis=1))
        out_ref[rows, low - start : high - start] = dot(diagonal[:, BLOCK:], work)
        out_ref[rows, low - start : low - start + BLOCK] = diagonal[:, :BLOCK]
        if low > start:
            out_ref[rows, : low - start] = jnp.zeros((BLOCK, low - start), jnp.float32)
        if high - start < out_ref.shape[1]:
            out_ref[rows, high - start :] = jnp.zeros((BLOCK, out_ref.shape[1] - high + start), jnp.float32)


def inverse_rows(blocks, i):
    per = blocks[0].shape[0]
    ref, at = blocks[i * BLOCK // per], i * BLOCK % per
    left = PANELS - i * BLOCK // per * per
    return ref[at : at + BLOCK, left : left + (i + 1) * BLOCK]


def last_factor_kernel(core_ref, own_ref, other_ref, panel_ref, *refs):
    blocks, basis_ref = refs[:-1], refs[-1]
    factor_kernel(PIECES - 1, core_ref, own_ref, other_ref, *blocks)
    for i in range(PANELS // BLOCK):
        upto = (i + 1) * BLOCK
        basis_ref[:, i * BLOCK : upto] = dot(panel_ref[:, :upto], inverse_rows(blocks, i), 1, 1)


def final_kernel(root_rows, core_ref, root_ref, *refs):
    ins, (out_hbm, factor_hbm), refs = refs[:6], refs[6:8], refs[8:]
    held, (out_ref, factor_ref, sems) = refs[:6], refs[6:]
    copies = [
        pltpu.make_async_copy(source, target, sems.at[i])
        for i, (source, target) in enumerate(zip(ins, held))
    ]
    for copy in copies:
        copy.start()
    upper_ref, lower_ref, own_ref, other_ref, basis_ref, front_ref = held
    blocks = (upper_ref, lower_ref)
    for copy in copies[:4]:
        copy.wait()
    sums = in_order(core_ref, own_ref[...], other_ref[...])
    coupled = jnp.concatenate(
        [dot(inverse_rows(blocks, i), sums[: (i + 1) * BLOCK, :]) for i in range(PANELS // BLOCK)],
        axis=0,
    )
    is_root = root_ref[0, 0] == 1
    per = PANELS // PIECES
    upper = jnp.concatenate(
        [
            jnp.concatenate(
                ([jnp.zeros((per, at), jnp.float32)] if at else []) + [ref[:, : PANELS - at]], axis=1
            )
            for ref, at in zip(blocks, range(0, PANELS, per))
        ],
        axis=0,
    )
    factor_ref[...] = jnp.where(is_root, upper, coupled) * (1.0 / root_rows)
    written = [pltpu.make_async_copy(factor_ref, factor_hbm, sems.at[6])]
    written[0].start()
    coupled_hi, coupled_mid, _ = split3(coupled)
    for copy in copies[4:]:
        copy.wait()
    half = out_ref.shape[0] // 2
    for i in range(2):
        rows = pl.ds(i * half, half)
        basis = basis_ref[rows, :]
        basis_hi, basis_mid, _ = split3(basis)
        update = dot_fast(basis_mid, coupled_hi) + dot_fast(basis_hi, coupled_mid)
        update = update + dot_fast(basis_hi, coupled_hi)
        out_ref[rows, :] = jnp.where(is_root, basis * root_rows, front_ref[rows, :] - update)
        written.append(
            pltpu.make_async_copy(out_ref.at[rows, :], out_hbm.at[rows, :], sems.at[7 + i])
        )
        written[-1].start()
    for copy in written:
        copy.wait()


def exchange(blocks, axis):
    return lax.all_to_all(blocks, axis, split_axis=0, concat_axis=0, tiled=True)


def swapped(x):
    return lax.ppermute(x, "core", [(0, 1), (1, 0)])


def summed(a, b):
    return call(add_kernel, f32(*a.shape), "add", 1 << 20, a, b, vmem=4)


def split_rows(x, n):
    return x.reshape(n, x.shape[0] // n, x.shape[1])


def merge_rows(x):
    return x.reshape(x.shape[0] * x.shape[1], x.shape[2])


def folded(x, n):
    return call(fold_kernel, f32(n, *x.shape[1:]), "fold", 1 << 20, x, vmem=6)


def on_device(front_in, child_block, child_rows, live_counts, column_map):
    rows_dev, cols_dev = front_in.shape
    owners, parts = lax.axis_size(ROW), lax.axis_size("col")
    chips = lax.axis_size(("z", "x"))
    count, child_width = child_block.shape
    capacity = count // owners
    core = lax.axis_index("core").astype(jnp.int32)
    col = lax.axis_index("col").astype(jnp.int32)
    is_root = (col == 0).astype(jnp.int32)
    halved = (f32(3 * PANELS // 2, BLOCK),) * 2
    local_cols = column_map % cols_dev

    step = capacity * (child_width // BLOCK) + 1
    sent = call(
        lambda *refs: pack_kernel(rows_dev, *refs), f32(owners * step, BLOCK), "pack", 1 << 20,
        child_block, child_rows.reshape(count // BLOCK, BLOCK), live_counts,
        ins=[HBM] * 3,
        vmem=56,
        scratch=[
            pltpu.VMEM((count, child_width), jnp.float32),
            pltpu.VMEM((count // BLOCK, BLOCK), jnp.int32),
            pltpu.VMEM((1, owners), jnp.int32),
            pltpu.SemaphoreType.DMA((3,)),
        ],
    )
    arrived = exchange(sent.reshape(owners, step, 1, BLOCK), ROW).reshape(owners * step, BLOCK)

    share = f32(rows_dev // parts, cols_dev)
    front, keep, send, *shares = call(
        lambda *refs: place_kernel(owners, *refs), [f32(rows_dev, cols_dev), *halved] + [share] * parts,
        "place", 4 << 30, front_in, arrived, local_cols.reshape(1, child_width), scalars=(core,),
        scratch=[pltpu.VMEM((3 * PANELS, BLOCK), jnp.float32)],
    )
    half = summed(keep, swapped(send))
    half, shares = lax.optimization_barrier((half, shares))
    far_first = sorted(range(1, parts), key=lambda k: -min(k, parts - k))
    sent_shares = [lax.ppermute(shares[k], "col", [(0, k)]) for k in far_first]
    grams = exchange(split_rows(half, chips), ("z", "x"))
    share_rows = rows_dev // parts * PANELS // BLOCK
    gram_rows = grams.shape[1]
    bundle = call(
        bundle_kernel, f32(parts, share_rows + gram_rows, BLOCK), "bundle", 1 << 20,
        grams, shares[0], *sent_shares, scalars=(is_root,), vmem=8,
    )
    bundle = exchange(bundle, "col")
    gram_share = call(
        gram_kernel, f32(chips, gram_rows, BLOCK), "gram_share", 1 << 20, bundle, vmem=6
    )
    own_gram = merge_rows(exchange(gram_share, ("z", "x")))
    other_gram = swapped(own_gram)

    panel, keep, send = call(
        product_kernel, (f32(rows_dev, PANELS),) + (f32(PANELS // 2, cols_dev),) * 2,
        "products", 2 << 30, front, bundle, scalars=(core,),
        scratch=[pltpu.VMEM((PANELS, cols_dev), jnp.float32)],
    )
    half = summed(keep, swapped(send))
    summands = exchange(split_rows(half, chips), ("z", "x"))

    block_shape = f32(PANELS // PIECES, 3 * PANELS // 2)
    upper = call(
        lambda *refs: factor_kernel(0, *refs), block_shape, "factor0", 10 << 30,
        own_gram, other_gram, scalars=(core,),
    )
    summands, upper = lax.optimization_barrier((summands, upper))
    own_sums = merge_rows(exchange(folded(summands, chips), ("z", "x")))
    lower, basis = call(
        last_factor_kernel, (block_shape, f32(rows_dev, PANELS)), "factor1", 12 << 30,
        own_gram, other_gram, panel, upper, scalars=(core,),
    )
    own_sums, basis = lax.optimization_barrier((own_sums, basis))
    other_sums = swapped(own_sums)
    whole = (rows_dev, cols_dev)
    ins = (upper, lower, own_sums, other_sums, basis, front)
    return call(
        lambda *refs: final_kernel(math.sqrt(rows_dev * owners), *refs),
        (f32(*whole), f32(PANELS, cols_dev)), "final", 4 << 30, *ins, scalars=(core, is_root),
        ins=[HBM] * len(ins), outs=(HBM, HBM), vmem=56,
        scratch=[pltpu.VMEM(x.shape, jnp.float32) for x in ins]
        + [pltpu.VMEM(whole, jnp.float32), pltpu.VMEM((PANELS, cols_dev), jnp.float32)]
        + [pltpu.SemaphoreType.DMA((9,))],
    )


def solution(mesh):
    row, col = mesh.shape["row"], mesh.shape["col"]
    fine = Mesh(mesh.devices.reshape(8, 4, row // 32, col), ROW + ("col",))
    return jax.shard_map(
        on_device,
        mesh=fine,
        in_specs=(P(ROW, "col"), P(ROW, "col"), P(ROW), P(ROW, None), P("col")),
        out_specs=(P(ROW, "col"), P(None, "col")),
        check_vma=False,
    )
```

```python
import math

import jax
import jax.numpy as jnp
from jax import lax
from jax.experimental import pallas as pl
from jax.experimental.pallas import tpu as pltpu
from jax.sharding import Mesh, PartitionSpec as P

PANELS = 512
BLOCK = 128
SUB = 64
PIECES = 2
ROW = ("z", "x", "core")
VMEM = pl.BlockSpec(memory_space=pltpu.VMEM)
SMEM = pl.BlockSpec(memory_space=pltpu.SMEM)
HBM = pl.BlockSpec(memory_space=pltpu.MemorySpace.HBM)


def dot_fast(a, b, ca=1, cb=0):
    return lax.dot_general(
        a, b, (((ca,), (cb,)), ((), ())), preferred_element_type=jnp.float32
    )


def dot(a, b, ca=1, cb=0):
    return lax.dot_general(
        a,
        b,
        (((ca,), (cb,)), ((), ())),
        precision=lax.Precision.HIGHEST,
        preferred_element_type=jnp.float32,
    )


def split3(a):
    hi = a.astype(jnp.bfloat16)
    rest = a - hi.astype(jnp.float32)
    mid = rest.astype(jnp.bfloat16)
    low = (rest - mid.astype(jnp.float32)).astype(jnp.bfloat16)
    return hi, mid, low


def f32(*shape):
    return jax.ShapeDtypeStruct(shape, jnp.float32)


def call(
    kernel, out_shape, name, flops, *args, scalars=(), scratch=(), vmem=14, ins=None, outs=None
):
    return pl.pallas_call(
        kernel,
        out_shape=out_shape,
        in_specs=[SMEM] * len(scalars) + (ins or [VMEM] * len(args)),
        out_specs=outs or jax.tree.map(lambda _: VMEM, out_shape),
        scratch_shapes=scratch,
        name=name,
        compiler_params=pltpu.CompilerParams(vmem_limit_bytes=vmem << 20),
        cost_estimate=pl.CostEstimate(flops=flops, bytes_accessed=4 << 20, transcendentals=0),
    )(*[s.reshape(1, 1) for s in scalars], *args)


def iota(shape, axis):
    return lax.broadcasted_iota(jnp.int32, shape, axis)


def hot(mask):
    return mask.astype(jnp.float32).astype(jnp.bfloat16)


def eye(size):
    return (iota((size, size), 0) == iota((size, size), 1)).astype(jnp.float32)


def pack_kernel(height, child_hbm, rows_hbm, live_hbm, out_ref, child_ref, rows_ref, live_ref, sems):
    copies = [
        pltpu.make_async_copy(live_hbm, live_ref, sems.at[0]),
        pltpu.make_async_copy(rows_hbm, rows_ref, sems.at[1]),
        pltpu.make_async_copy(child_hbm, child_ref, sems.at[2]),
    ]
    for copy in copies:
        copy.start()
    copies[0].wait()
    copies[1].wait()
    count, width = child_ref.shape
    owners = live_ref.shape[1]
    capacity, lanes = count // owners, rows_ref.shape[1]
    live = jnp.broadcast_to(live_ref[...].astype(jnp.float32), (count, owners))
    owner = lax.div(iota((count, owners), 0), jnp.int32(capacity))
    live = jnp.sum(jnp.where(owner == iota((count, owners), 1), live, 0.0), axis=1, keepdims=True)
    slot = lax.rem(iota((count, 1), 0), jnp.int32(capacity))
    local = lax.rem(rows_ref[...], jnp.int32(height)).astype(jnp.float32)
    identity = eye(lanes)
    rows = jnp.concatenate(
        [
            jnp.sum(jnp.broadcast_to(local[g : g + 1, :], (lanes, lanes)) * identity, axis=1, keepdims=True)
            for g in range(count // lanes)
        ],
        axis=0,
    )
    places = jnp.where(slot.astype(jnp.float32) < live, rows, -1.0)
    spread = jnp.where(iota((count, lanes), 1) == slot, jnp.broadcast_to(places, (count, lanes)), 0.0)
    places = jnp.sum(spread.reshape(owners, capacity, lanes), axis=1)
    copies[2].wait()
    step = out_ref.shape[0] // owners
    for s in range(owners):
        for h in range(width // BLOCK):
            at = s * step + h * capacity
            out_ref[at : at + capacity, :] = child_ref[
                s * capacity : (s + 1) * capacity, h * BLOCK : (h + 1) * BLOCK
            ]
        out_ref[s * step + step - 1 : s * step + step, :] = places[s : s + 1, :]


def unpacked(ref, owners, capacity, width):
    step = ref.shape[0] // owners
    rows = jnp.concatenate(
        [
            jnp.concatenate(
                [
                    ref[s * step + h * capacity : s * step + (h + 1) * capacity, :]
                    for s in range(owners)
                ],
                axis=0,
            )
            for h in range(width // BLOCK)
        ],
        axis=1,
    )
    shape = (owners * capacity, BLOCK)
    places = jnp.concatenate(
        [
            jnp.broadcast_to(ref[s * step + step - 1 : s * step + step, :], (capacity, BLOCK))
            for s in range(owners)
        ],
        axis=0,
    )
    own = iota(shape, 1) == lax.rem(iota(shape, 0), jnp.int32(capacity))
    places = jnp.sum(jnp.where(own, places, 0.0), axis=1, keepdims=True)
    return rows, places.astype(jnp.int32)


def placed(front, rows, targets, cols):
    height, width = front.shape
    count, child_width = rows.shape
    col_hot = hot(iota((width, child_width), 0) == cols)
    row_hot = hot(iota((count, height), 1) == targets)
    total = front
    for term in split3(rows):
        spread = dot_fast(term, col_hot, 1, 1).astype(jnp.bfloat16)
        total = total + dot_fast(row_hot, spread, 0, 0)
    return total


def bundle_kernel(root_ref, own_ref, *refs):
    arrived, out_ref = refs[:-1], refs[-1]
    share = jnp.where(root_ref[0, 0] == 1, own_ref[...], total([ref[...] for ref in arrived]))
    for i in range(out_ref.shape[0]):
        out_ref[i] = share


def gram_share_kernel(grams_ref, out_ref):
    out_ref[...] = total([grams_ref[i] for i in range(grams_ref.shape[0])])


def chosen_kernel(root_ref, own_ref, *refs):
    arrived, out_ref = refs[:-1], refs[-1]
    out_ref[...] = jnp.where(root_ref[0, 0] == 1, own_ref[...], total([ref[...] for ref in arrived]))


def line_kernel(x_ref, *refs):
    shares, out_ref = refs[:-1], refs[-1]
    height, n = shares[0].shape[0], len(shares)
    for k, ref in enumerate(shares):
        source = lax.rem(x_ref[0, 0] + (n - k), jnp.int32(n))
        for i in range(out_ref.shape[0]):
            out_ref[i, pl.ds(pl.multiple_of(source * height, 8), height), :] = ref[...]


def total(terms):
    while len(terms) > 1:
        pairs = [a + b for a, b in zip(terms[::2], terms[1::2])]
        terms = pairs + terms[len(pairs) * 2 :]
    return terms[0]


def add_kernel(a_ref, b_ref, out_ref):
    out_ref[...] = a_ref[...] + b_ref[...]


def fold_kernel(x_ref, out_ref):
    x = total([x_ref[i] for i in range(x_ref.shape[0])])
    for i in range(out_ref.shape[0]):
        out_ref[i] = x


def halves(core_ref, whole_ref, keep_ref, send_ref):
    height = keep_ref.shape[0]
    core = core_ref[0, 0]
    keep_ref[...] = whole_ref[pl.ds(pl.multiple_of(core * height, height), height), :]
    send_ref[...] = whole_ref[pl.ds(pl.multiple_of((1 - core) * height, height), height), :]


def gram_place(i, j):
    if i < 2:
        return (2 * j + i) * BLOCK
    return (2 * PANELS // BLOCK + 2 * (j - 2) + i - 2) * BLOCK


def place_kernel(
    owners, core_ref, front_ref, arrived_ref, cols_ref, out_ref, keep_ref, send_ref, *refs
):
    share_refs, whole_ref = refs[:-1], refs[-1]
    width = cols_ref.shape[1]
    capacity = (arrived_ref.shape[0] // owners - 1) // (width // BLOCK)
    rows, places = unpacked(arrived_ref, owners, capacity, width)
    front = placed(front_ref[...], rows, places, cols_ref[...])
    out_ref[...] = front
    height = share_refs[0].shape[0]
    for k, ref in enumerate(share_refs):
        ref[...] = front[k * height : (k + 1) * height, :]
    half = PANELS // 2
    for first in range(2):
        cols = slice(half * first, PANELS)
        product = dot(front[:, half * first : half * (first + 1)], front[:, cols], 0, 0)
        for i in range(2):
            for j in range(2 * first, PANELS // BLOCK):
                at = gram_place(2 * first + i, j)
                left = (j - 2 * first) * BLOCK
                whole_ref[at : at + BLOCK, :] = product[i * BLOCK : (i + 1) * BLOCK, left : left + BLOCK]
    halves(core_ref, whole_ref, keep_ref, send_ref)


def product_kernel(core_ref, front_ref, bundle_ref, panel_ref, keep_ref, send_ref, whole_ref):
    parts = bundle_ref.shape[0]
    height = panel_ref.shape[0] // parts
    for k in range(parts):
        panel_ref[k * height : (k + 1) * height, :] = bundle_ref[k]
    whole_ref[...] = dot(panel_ref[...], front_ref[...], 0, 0)
    halves(core_ref, whole_ref, keep_ref, send_ref)


def factor_diagonal(block):
    width = block.shape[1]
    done = []
    rest = block
    at_narrow, at_wide = iota((8, BLOCK), 0), iota((8, width), 0)
    count = SUB // 8
    for sub in range(BLOCK // SUB):
        groups = [rest[8 * g : 8 * g + 8, :] for g in range(count)]
        for p in range(count):
            first = SUB * sub + 8 * p
            spread = {
                (g, k): jnp.broadcast_to(groups[g][:, first + k : first + k + 1], (8, BLOCK))
                for g in range(p, count)
                for k in range(8)
            }
            for j in range(8):
                scale = lax.rsqrt(jnp.broadcast_to(spread[p, j][j : j + 1, :], (8, BLOCK)))
                factor = {g: spread[g, j] * scale for g in range(p, count)}
                factor[p] = jnp.where(at_narrow > j, factor[p], 0.0)
                for k in range(j + 1, 8):
                    pivot = jnp.broadcast_to(spread[p, k][j : j + 1, :], (8, BLOCK)) * scale
                    for g in range(p, count):
                        spread[g, k] = spread[g, k] - factor[g] * pivot
                wide = jnp.concatenate([scale] * (width // BLOCK), axis=1)
                row = jnp.broadcast_to(groups[p][j : j + 1, :], (8, width)) * wide
                for g in range(p, count):
                    updated = groups[g] - jnp.concatenate([factor[g]] * (width // BLOCK), axis=1) * row
                    groups[g] = jnp.where(at_wide == j, row, updated) if g == p else updated
        rows = jnp.concatenate(groups, axis=0)
        done.append(rows)
        if sub + 1 < BLOCK // SUB:
            rest = rest[SUB:, :] - dot(rows[:, SUB * (sub + 1) : BLOCK], rows, 0, 0)
    return jnp.concatenate(done, axis=0)


def in_order(core_ref, own, other):
    first = core_ref[0, 0] == 0
    return jnp.concatenate(
        [jnp.where(first, own, other), jnp.where(first, other, own)], axis=0
    )


def factor_kernel(piece, core_ref, own_ref, other_ref, *refs):
    above, out_ref = refs[:-1], refs[-1]
    n = PANELS
    per = n // BLOCK // PIECES
    gram = in_order(core_ref, own_ref[...], other_ref[...])
    identity = eye(BLOCK)

    def rows_of(block):
        at = block % per * BLOCK
        start = block // per * per * BLOCK
        return (*above, out_ref)[block // per], slice(at, at + BLOCK), start

    for k in range(piece * per, (piece + 1) * per):
        _, rows, start = rows_of(k)
        low, high = k * BLOCK, n + (k + 1) * BLOCK
        starts = [gram_place(k, j) for j in range(k, n // BLOCK)]
        pad = [jnp.zeros((BLOCK, low), jnp.float32)] if k else []
        work = jnp.concatenate([gram[at : at + BLOCK, :] for at in starts] + pad + [identity], axis=1)
        for upper in range(k):
            ref, at, shift = rows_of(upper)
            end = min(high, shift + ref.shape[1])
            factor = dot(ref[at, low - shift : low - shift + BLOCK], ref[at, low - shift : end - shift], 0, 0)
            if end < high:
                factor = jnp.concatenate([factor, jnp.zeros((BLOCK, high - end), jnp.float32)], axis=1)
            work = work - factor
        diagonal = factor_diagonal(jnp.concatenate([work[:, :BLOCK], identity], axis=1))
        out_ref[rows, low - start : high - start] = dot(diagonal[:, BLOCK:], work)
        out_ref[rows, low - start : low - start + BLOCK] = diagonal[:, :BLOCK]
        if low > start:
            out_ref[rows, : low - start] = jnp.zeros((BLOCK, low - start), jnp.float32)
        if high - start < out_ref.shape[1]:
            out_ref[rows, high - start :] = jnp.zeros((BLOCK, out_ref.shape[1] - high + start), jnp.float32)


def inverse_rows(blocks, i):
    per = blocks[0].shape[0]
    ref, at = blocks[i * BLOCK // per], i * BLOCK % per
    left = PANELS - i * BLOCK // per * per
    return ref[at : at + BLOCK, left : left + (i + 1) * BLOCK]


def last_factor_kernel(core_ref, own_ref, other_ref, panel_ref, *refs):
    blocks, basis_ref = refs[:-1], refs[-1]
    factor_kernel(PIECES - 1, core_ref, own_ref, other_ref, *blocks)
    for i in range(PANELS // BLOCK):
        upto = (i + 1) * BLOCK
        basis_ref[:, i * BLOCK : upto] = dot(panel_ref[:, :upto], inverse_rows(blocks, i), 1, 1)


def final_kernel(root_rows, core_ref, root_ref, *refs):
    ins, (out_hbm, factor_hbm), refs = refs[:6], refs[6:8], refs[8:]
    held, (out_ref, factor_ref, sems) = refs[:6], refs[6:]
    copies = [
        pltpu.make_async_copy(source, target, sems.at[i])
        for i, (source, target) in enumerate(zip(ins, held))
    ]
    for copy in copies:
        copy.start()
    upper_ref, lower_ref, own_ref, other_ref, basis_ref, front_ref = held
    blocks = (upper_ref, lower_ref)
    for copy in copies[:4]:
        copy.wait()
    sums = in_order(core_ref, own_ref[...], other_ref[...])
    coupled = jnp.concatenate(
        [dot(inverse_rows(blocks, i), sums[: (i + 1) * BLOCK, :]) for i in range(PANELS // BLOCK)],
        axis=0,
    )
    is_root = root_ref[0, 0] == 1
    per = PANELS // PIECES
    upper = jnp.concatenate(
        [
            jnp.concatenate(
                ([jnp.zeros((per, at), jnp.float32)] if at else []) + [ref[:, : PANELS - at]], axis=1
            )
            for ref, at in zip(blocks, range(0, PANELS, per))
        ],
        axis=0,
    )
    factor_ref[...] = jnp.where(is_root, upper, coupled) * (1.0 / root_rows)
    written = [pltpu.make_async_copy(factor_ref, factor_hbm, sems.at[6])]
    written[0].start()
    coupled_hi, coupled_mid, _ = split3(coupled)
    for copy in copies[4:]:
        copy.wait()
    half = out_ref.shape[0] // 2
    for i in range(2):
        rows = pl.ds(i * half, half)
        basis = basis_ref[rows, :]
        basis_hi, basis_mid, _ = split3(basis)
        update = dot_fast(basis_mid, coupled_hi) + dot_fast(basis_hi, coupled_mid)
        update = update + dot_fast(basis_hi, coupled_hi)
        out_ref[rows, :] = jnp.where(is_root, basis * root_rows, front_ref[rows, :] - update)
        written.append(
            pltpu.make_async_copy(out_ref.at[rows, :], out_hbm.at[rows, :], sems.at[7 + i])
        )
        written[-1].start()
    for copy in written:
        copy.wait()


def exchange(blocks, axis):
    return lax.all_to_all(blocks, axis, split_axis=0, concat_axis=0, tiled=True)


def swapped(x):
    return lax.ppermute(x, "core", [(0, 1), (1, 0)])


def summed(a, b):
    return call(add_kernel, f32(*a.shape), "add", 1 << 20, a, b, vmem=4)


def split_rows(x, n):
    return x.reshape(n, x.shape[0] // n, x.shape[1])


def merge_rows(x):
    return x.reshape(x.shape[0] * x.shape[1], x.shape[2])


def folded(x, n):
    return call(fold_kernel, f32(n, *x.shape[1:]), "fold", 1 << 20, x, vmem=6)


def on_device(front_in, child_block, child_rows, live_counts, column_map):
    rows_dev, cols_dev = front_in.shape
    owners, parts = lax.axis_size(ROW), lax.axis_size("col")
    chips = lax.axis_size(("z", "x"))
    count, child_width = child_block.shape
    capacity = count // owners
    core = lax.axis_index("core").astype(jnp.int32)
    col = lax.axis_index("col").astype(jnp.int32)
    is_root = (col == 0).astype(jnp.int32)
    halved = (f32(3 * PANELS // 2, BLOCK),) * 2
    local_cols = column_map % cols_dev

    step = capacity * (child_width // BLOCK) + 1
    sent = call(
        lambda *refs: pack_kernel(rows_dev, *refs), f32(owners * step, BLOCK), "pack", 1 << 20,
        child_block, child_rows.reshape(count // BLOCK, BLOCK), live_counts,
        ins=[HBM] * 3,
        vmem=56,
        scratch=[
            pltpu.VMEM((count, child_width), jnp.float32),
            pltpu.VMEM((count // BLOCK, BLOCK), jnp.int32),
            pltpu.VMEM((1, owners), jnp.int32),
            pltpu.SemaphoreType.DMA((3,)),
        ],
    )
    arrived = exchange(sent.reshape(owners, step, 1, BLOCK), ROW).reshape(owners * step, BLOCK)

    share = f32(rows_dev // parts, cols_dev)
    front, keep, send, *shares = call(
        lambda *refs: place_kernel(owners, *refs), [f32(rows_dev, cols_dev), *halved] + [share] * parts,
        "place", 4 << 30, front_in, arrived, local_cols.reshape(1, child_width), scalars=(core,),
        scratch=[pltpu.VMEM((3 * PANELS, BLOCK), jnp.float32)],
    )
    half = summed(keep, swapped(send))
    half, shares = lax.optimization_barrier((half, shares))
    far_first = sorted(range(1, parts), key=lambda k: -min(k, parts - k))
    sent_shares = [lax.ppermute(shares[k], "col", [(0, k)]) for k in far_first]
    grams = exchange(split_rows(half, chips), ("z", "x"))
    bundle = call(
        bundle_kernel, f32(parts, rows_dev // parts, PANELS), "bundle", 1 << 20,
        shares[0], *sent_shares, scalars=(is_root,), vmem=8,
    )
    grams, bundle = lax.optimization_barrier((grams, bundle))
    bundle = exchange(bundle, "col")
    gram_share = f32(*grams.shape[1:])
    reduced = call(gram_share_kernel, gram_share, "gram_share", 1 << 20, grams, vmem=6)
    sent_grams = [lax.ppermute(reduced, "col", [(0, k)]) for k in far_first]
    reduced = call(
        chosen_kernel, gram_share, "chosen", 1 << 20, reduced, *sent_grams, scalars=(is_root,), vmem=4
    )
    line, column = lax.axis_size("x"), lax.axis_size("z")
    along_x = [reduced] + [
        lax.ppermute(reduced, "x", [(i, (i + k) % line) for i in range(line)]) for k in range(1, line)
    ]
    gram_line = call(
        line_kernel, f32(column, line * grams.shape[1], BLOCK), "line", 1 << 20, *along_x,
        scalars=(lax.axis_index("x").astype(jnp.int32),), vmem=6,
    )
    bundle, gram_line = lax.optimization_barrier((bundle, gram_line))
    own_gram = merge_rows(exchange(gram_line, "z"))

    panel, keep, send = call(
        product_kernel, (f32(rows_dev, PANELS),) + (f32(PANELS // 2, cols_dev),) * 2,
        "products", 2 << 30, front, bundle, scalars=(core,),
        scratch=[pltpu.VMEM((PANELS, cols_dev), jnp.float32)],
    )
    half = summed(keep, swapped(send))
    half, own_gram = lax.optimization_barrier((half, own_gram))
    other_gram = swapped(own_gram)
    summands = exchange(split_rows(half, chips), ("z", "x"))

    block_shape = f32(PANELS // PIECES, 3 * PANELS // 2)
    upper = call(
        lambda *refs: factor_kernel(0, *refs), block_shape, "factor0", 10 << 30,
        own_gram, other_gram, scalars=(core,),
    )
    summands, upper = lax.optimization_barrier((summands, upper))
    own_sums = merge_rows(exchange(folded(summands, chips), ("z", "x")))
    lower, basis = call(
        last_factor_kernel, (block_shape, f32(rows_dev, PANELS)), "factor1", 12 << 30,
        own_gram, other_gram, panel, upper, scalars=(core,),
    )
    own_sums, basis = lax.optimization_barrier((own_sums, basis))
    other_sums = swapped(own_sums)
    whole = (rows_dev, cols_dev)
    ins = (upper, lower, own_sums, other_sums, basis, front)
    return call(
        lambda *refs: final_kernel(math.sqrt(rows_dev * owners), *refs),
        (f32(*whole), f32(PANELS, cols_dev)), "final", 4 << 30, *ins, scalars=(core, is_root),
        ins=[HBM] * len(ins), outs=(HBM, HBM), vmem=56,
        scratch=[pltpu.VMEM(x.shape, jnp.float32) for x in ins]
        + [pltpu.VMEM(whole, jnp.float32), pltpu.VMEM((PANELS, cols_dev), jnp.float32)]
        + [pltpu.SemaphoreType.DMA((9,))],
    )


def solution(mesh):
    row, col = mesh.shape["row"], mesh.shape["col"]
    fine = Mesh(mesh.devices.reshape(8, 4, row // 32, col), ROW + ("col",))
    return jax.shard_map(
        on_device,
        mesh=fine,
        in_specs=(P(ROW, "col"), P(ROW, "col"), P(ROW), P(ROW, None), P("col")),
        out_specs=(P(ROW, "col"), P(None, "col")),
        check_vma=False,
    )
```

```python
import math

import jax
import jax.numpy as jnp
from jax import lax
from jax.experimental import pallas as pl
from jax.experimental.pallas import tpu as pltpu
from jax.sharding import Mesh, PartitionSpec as P

PANELS = 512
BLOCK = 128
SUB = 64
PIECES = 2
ROW = ("z", "x", "core")
VMEM = pl.BlockSpec(memory_space=pltpu.VMEM)
SMEM = pl.BlockSpec(memory_space=pltpu.SMEM)
HBM = pl.BlockSpec(memory_space=pltpu.MemorySpace.HBM)


def dot_fast(a, b, ca=1, cb=0):
    return lax.dot_general(
        a, b, (((ca,), (cb,)), ((), ())), preferred_element_type=jnp.float32
    )


def dot(a, b, ca=1, cb=0):
    return lax.dot_general(
        a,
        b,
        (((ca,), (cb,)), ((), ())),
        precision=lax.Precision.HIGHEST,
        preferred_element_type=jnp.float32,
    )


def split3(a):
    hi = a.astype(jnp.bfloat16)
    rest = a - hi.astype(jnp.float32)
    mid = rest.astype(jnp.bfloat16)
    low = (rest - mid.astype(jnp.float32)).astype(jnp.bfloat16)
    return hi, mid, low


def f32(*shape):
    return jax.ShapeDtypeStruct(shape, jnp.float32)


def call(
    kernel, out_shape, name, flops, *args, scalars=(), scratch=(), vmem=14, ins=None, outs=None
):
    return pl.pallas_call(
        kernel,
        out_shape=out_shape,
        in_specs=[SMEM] * len(scalars) + (ins or [VMEM] * len(args)),
        out_specs=outs or jax.tree.map(lambda _: VMEM, out_shape),
        scratch_shapes=scratch,
        name=name,
        compiler_params=pltpu.CompilerParams(vmem_limit_bytes=vmem << 20),
        cost_estimate=pl.CostEstimate(flops=flops, bytes_accessed=4 << 20, transcendentals=0),
    )(*[s.reshape(1, 1) for s in scalars], *args)


def iota(shape, axis):
    return lax.broadcasted_iota(jnp.int32, shape, axis)


def hot(mask):
    return mask.astype(jnp.float32).astype(jnp.bfloat16)


def eye(size):
    return (iota((size, size), 0) == iota((size, size), 1)).astype(jnp.float32)


def pack_kernel(height, child_hbm, rows_hbm, live_hbm, out_ref, child_ref, rows_ref, live_ref, sems):
    copies = [
        pltpu.make_async_copy(live_hbm, live_ref, sems.at[0]),
        pltpu.make_async_copy(rows_hbm, rows_ref, sems.at[1]),
        pltpu.make_async_copy(child_hbm, child_ref, sems.at[2]),
    ]
    for copy in copies:
        copy.start()
    copies[0].wait()
    copies[1].wait()
    count, width = child_ref.shape
    owners = live_ref.shape[1]
    capacity, lanes = count // owners, rows_ref.shape[1]
    live = jnp.broadcast_to(live_ref[...].astype(jnp.float32), (count, owners))
    owner = lax.div(iota((count, owners), 0), jnp.int32(capacity))
    live = jnp.sum(jnp.where(owner == iota((count, owners), 1), live, 0.0), axis=1, keepdims=True)
    slot = lax.rem(iota((count, 1), 0), jnp.int32(capacity))
    local = lax.rem(rows_ref[...], jnp.int32(height)).astype(jnp.float32)
    identity = eye(lanes)
    rows = jnp.concatenate(
        [
            jnp.sum(jnp.broadcast_to(local[g : g + 1, :], (lanes, lanes)) * identity, axis=1, keepdims=True)
            for g in range(count // lanes)
        ],
        axis=0,
    )
    places = jnp.where(slot.astype(jnp.float32) < live, rows, -1.0)
    spread = jnp.where(iota((count, lanes), 1) == slot, jnp.broadcast_to(places, (count, lanes)), 0.0)
    places = jnp.sum(spread.reshape(owners, capacity, lanes), axis=1)
    copies[2].wait()
    step = out_ref.shape[0] // owners
    for s in range(owners):
        for h in range(width // BLOCK):
            at = s * step + h * capacity
            out_ref[at : at + capacity, :] = child_ref[
                s * capacity : (s + 1) * capacity, h * BLOCK : (h + 1) * BLOCK
            ]
        out_ref[s * step + step - 1 : s * step + step, :] = places[s : s + 1, :]


def unpacked(ref, owners, capacity, width):
    step = ref.shape[0] // owners
    rows = jnp.concatenate(
        [
            jnp.concatenate(
                [
                    ref[s * step + h * capacity : s * step + (h + 1) * capacity, :]
                    for s in range(owners)
                ],
                axis=0,
            )
            for h in range(width // BLOCK)
        ],
        axis=1,
    )
    shape = (owners * capacity, BLOCK)
    places = jnp.concatenate(
        [
            jnp.broadcast_to(ref[s * step + step - 1 : s * step + step, :], (capacity, BLOCK))
            for s in range(owners)
        ],
        axis=0,
    )
    own = iota(shape, 1) == lax.rem(iota(shape, 0), jnp.int32(capacity))
    places = jnp.sum(jnp.where(own, places, 0.0), axis=1, keepdims=True)
    return rows, places.astype(jnp.int32)


def placed(front, rows, targets, cols):
    height, width = front.shape
    count, child_width = rows.shape
    col_hot = hot(iota((width, child_width), 0) == cols)
    row_hot = hot(iota((count, height), 1) == targets)
    total = front
    for term in split3(rows):
        spread = dot_fast(term, col_hot, 1, 1).astype(jnp.bfloat16)
        total = total + dot_fast(row_hot, spread, 0, 0)
    return total


def bundle_kernel(root_ref, grams_ref, own_ref, *refs):
    arrived, out_ref = refs[:-1], refs[-1]
    share = total([ref[...] for ref in arrived])
    share = jnp.where(root_ref[0, 0] == 1, own_ref[...], share)
    gram = total([grams_ref[i] for i in range(grams_ref.shape[0])])
    height = share.shape[0]
    for i in range(out_ref.shape[0]):
        for lanes in range(share.shape[1] // BLOCK):
            out_ref[i, lanes * height : (lanes + 1) * height, :] = share[
                :, lanes * BLOCK : (lanes + 1) * BLOCK
            ]
        out_ref[i, share.shape[1] // BLOCK * height :, :] = gram


def total(terms):
    while len(terms) > 1:
        pairs = [a + b for a, b in zip(terms[::2], terms[1::2])]
        terms = pairs + terms[len(pairs) * 2 :]
    return terms[0]


def add_kernel(a_ref, b_ref, out_ref):
    out_ref[...] = a_ref[...] + b_ref[...]


def fold_kernel(x_ref, out_ref):
    x = total([x_ref[i] for i in range(x_ref.shape[0])])
    for i in range(out_ref.shape[0]):
        out_ref[i] = x


def gram_kernel(bundle_ref, out_ref):
    height = out_ref.shape[1]
    for i in range(out_ref.shape[0]):
        out_ref[i] = bundle_ref[0, bundle_ref.shape[1] - height :, :]


def halves(core_ref, whole_ref, keep_ref, send_ref):
    height = keep_ref.shape[0]
    core = core_ref[0, 0]
    keep_ref[...] = whole_ref[pl.ds(pl.multiple_of(core * height, height), height), :]
    send_ref[...] = whole_ref[pl.ds(pl.multiple_of((1 - core) * height, height), height), :]


def gram_place(i, j):
    if i < 2:
        return (2 * j + i) * BLOCK
    return (2 * PANELS // BLOCK + 2 * (j - 2) + i - 2) * BLOCK


def place_kernel(
    owners, core_ref, front_ref, arrived_ref, cols_ref, out_ref, keep_ref, send_ref, *refs
):
    share_refs, whole_ref = refs[:-1], refs[-1]
    width = cols_ref.shape[1]
    capacity = (arrived_ref.shape[0] // owners - 1) // (width // BLOCK)
    rows, places = unpacked(arrived_ref, owners, capacity, width)
    front = placed(front_ref[...], rows, places, cols_ref[...])
    out_ref[...] = front
    height = share_refs[0].shape[0]
    for k, ref in enumerate(share_refs):
        ref[...] = front[k * height : (k + 1) * height, :]
    half = PANELS // 2
    for first in range(2):
        cols = slice(half * first, PANELS)
        product = dot(front[:, half * first : half * (first + 1)], front[:, cols], 0, 0)
        for i in range(2):
            for j in range(2 * first, PANELS // BLOCK):
                at = gram_place(2 * first + i, j)
                left = (j - 2 * first) * BLOCK
                whole_ref[at : at + BLOCK, :] = product[i * BLOCK : (i + 1) * BLOCK, left : left + BLOCK]
    halves(core_ref, whole_ref, keep_ref, send_ref)


def product_kernel(core_ref, front_ref, bundle_ref, panel_ref, keep_ref, send_ref, whole_ref):
    parts = bundle_ref.shape[0]
    height = panel_ref.shape[0] // parts
    for k in range(parts):
        for lanes in range(panel_ref.shape[1] // BLOCK):
            panel_ref[k * height : (k + 1) * height, lanes * BLOCK : (lanes + 1) * BLOCK] = bundle_ref[
                k, lanes * height : (lanes + 1) * height, :
            ]
    whole_ref[...] = dot(panel_ref[...], front_ref[...], 0, 0)
    halves(core_ref, whole_ref, keep_ref, send_ref)


def factor_diagonal(block):
    width = block.shape[1]
    done = []
    rest = block
    at_narrow, at_wide = iota((8, BLOCK), 0), iota((8, width), 0)
    count = SUB // 8
    for sub in range(BLOCK // SUB):
        groups = [rest[8 * g : 8 * g + 8, :] for g in range(count)]
        for p in range(count):
            first = SUB * sub + 8 * p
            spread = {
                (g, k): jnp.broadcast_to(groups[g][:, first + k : first + k + 1], (8, BLOCK))
                for g in range(p, count)
                for k in range(8)
            }
            for j in range(8):
                scale = lax.rsqrt(jnp.broadcast_to(spread[p, j][j : j + 1, :], (8, BLOCK)))
                factor = {g: spread[g, j] * scale for g in range(p, count)}
                factor[p] = jnp.where(at_narrow > j, factor[p], 0.0)
                for k in range(j + 1, 8):
                    pivot = jnp.broadcast_to(spread[p, k][j : j + 1, :], (8, BLOCK)) * scale
                    for g in range(p, count):
                        spread[g, k] = spread[g, k] - factor[g] * pivot
                wide = jnp.concatenate([scale] * (width // BLOCK), axis=1)
                row = jnp.broadcast_to(groups[p][j : j + 1, :], (8, width)) * wide
                for g in range(p, count):
                    updated = groups[g] - jnp.concatenate([factor[g]] * (width // BLOCK), axis=1) * row
                    groups[g] = jnp.where(at_wide == j, row, updated) if g == p else updated
        rows = jnp.concatenate(groups, axis=0)
        done.append(rows)
        if sub + 1 < BLOCK // SUB:
            rest = rest[SUB:, :] - dot(rows[:, SUB * (sub + 1) : BLOCK], rows, 0, 0)
    return jnp.concatenate(done, axis=0)


def in_order(core_ref, own, other):
    first = core_ref[0, 0] == 0
    return jnp.concatenate(
        [jnp.where(first, own, other), jnp.where(first, other, own)], axis=0
    )


def factor_kernel(piece, core_ref, own_ref, other_ref, *refs):
    above, out_ref = refs[:-1], refs[-1]
    n = PANELS
    per = n // BLOCK // PIECES
    gram = in_order(core_ref, own_ref[...], other_ref[...])
    identity = eye(BLOCK)

    def rows_of(block):
        at = block % per * BLOCK
        start = block // per * per * BLOCK
        return (*above, out_ref)[block // per], slice(at, at + BLOCK), start

    for k in range(piece * per, (piece + 1) * per):
        _, rows, start = rows_of(k)
        low, high = k * BLOCK, n + (k + 1) * BLOCK
        starts = [gram_place(k, j) for j in range(k, n // BLOCK)]
        pad = [jnp.zeros((BLOCK, low), jnp.float32)] if k else []
        work = jnp.concatenate([gram[at : at + BLOCK, :] for at in starts] + pad + [identity], axis=1)
        for upper in range(k):
            ref, at, shift = rows_of(upper)
            end = min(high, shift + ref.shape[1])
            factor = dot(ref[at, low - shift : low - shift + BLOCK], ref[at, low - shift : end - shift], 0, 0)
            if end < high:
                factor = jnp.concatenate([factor, jnp.zeros((BLOCK, high - end), jnp.float32)], axis=1)
            work = work - factor
        diagonal = factor_diagonal(jnp.concatenate([work[:, :BLOCK], identity], axis=1))
        out_ref[rows, low - start : high - start] = dot(diagonal[:, BLOCK:], work)
        out_ref[rows, low - start : low - start + BLOCK] = diagonal[:, :BLOCK]
        if low > start:
            out_ref[rows, : low - start] = jnp.zeros((BLOCK, low - start), jnp.float32)
        if high - start < out_ref.shape[1]:
            out_ref[rows, high - start :] = jnp.zeros((BLOCK, out_ref.shape[1] - high + start), jnp.float32)


def inverse_rows(blocks, i):
    per = blocks[0].shape[0]
    ref, at = blocks[i * BLOCK // per], i * BLOCK % per
    left = PANELS - i * BLOCK // per * per
    return ref[at : at + BLOCK, left : left + (i + 1) * BLOCK]


def last_factor_kernel(core_ref, own_ref, other_ref, panel_ref, *refs):
    blocks, basis_ref = refs[:-1], refs[-1]
    factor_kernel(PIECES - 1, core_ref, own_ref, other_ref, *blocks)
    for i in range(PANELS // BLOCK):
        upto = (i + 1) * BLOCK
        basis_ref[:, i * BLOCK : upto] = dot(panel_ref[:, :upto], inverse_rows(blocks, i), 1, 1)


def final_kernel(root_rows, core_ref, root_ref, *refs):
    ins, (out_hbm, factor_hbm), refs = refs[:6], refs[6:8], refs[8:]
    held, (out_ref, factor_ref, sems) = refs[:6], refs[6:]
    copies = [
        pltpu.make_async_copy(source, target, sems.at[i])
        for i, (source, target) in enumerate(zip(ins, held))
    ]
    for copy in copies:
        copy.start()
    upper_ref, lower_ref, own_ref, other_ref, basis_ref, front_ref = held
    blocks = (upper_ref, lower_ref)
    for copy in copies[:4]:
        copy.wait()
    sums = in_order(core_ref, own_ref[...], other_ref[...])
    coupled = jnp.concatenate(
        [dot(inverse_rows(blocks, i), sums[: (i + 1) * BLOCK, :]) for i in range(PANELS // BLOCK)],
        axis=0,
    )
    is_root = root_ref[0, 0] == 1
    per = PANELS // PIECES
    upper = jnp.concatenate(
        [
            jnp.concatenate(
                ([jnp.zeros((per, at), jnp.float32)] if at else []) + [ref[:, : PANELS - at]], axis=1
            )
            for ref, at in zip(blocks, range(0, PANELS, per))
        ],
        axis=0,
    )
    factor_ref[...] = jnp.where(is_root, upper, coupled) * (1.0 / root_rows)
    written = [pltpu.make_async_copy(factor_ref, factor_hbm, sems.at[6])]
    written[0].start()
    coupled_hi, coupled_mid, _ = split3(coupled)
    for copy in copies[4:]:
        copy.wait()
    half = out_ref.shape[0] // 2
    for i in range(2):
        rows = pl.ds(i * half, half)
        basis = basis_ref[rows, :]
        basis_hi, basis_mid, _ = split3(basis)
        update = dot_fast(basis_mid, coupled_hi) + dot_fast(basis_hi, coupled_mid)
        update = update + dot_fast(basis_hi, coupled_hi)
        out_ref[rows, :] = jnp.where(is_root, basis * root_rows, front_ref[rows, :] - update)
        written.append(
            pltpu.make_async_copy(out_ref.at[rows, :], out_hbm.at[rows, :], sems.at[7 + i])
        )
        written[-1].start()
    for copy in written:
        copy.wait()


def exchange(blocks, axis):
    return lax.all_to_all(blocks, axis, split_axis=0, concat_axis=0, tiled=True)


def swapped(x):
    return lax.ppermute(x, "core", [(0, 1), (1, 0)])


def summed(a, b):
    return call(add_kernel, f32(*a.shape), "add", 1 << 20, a, b, vmem=4)


def split_rows(x, n):
    return x.reshape(n, x.shape[0] // n, x.shape[1])


def merge_rows(x):
    return x.reshape(x.shape[0] * x.shape[1], x.shape[2])


def folded(x, n):
    return call(fold_kernel, f32(n, *x.shape[1:]), "fold", 1 << 20, x, vmem=6)


def on_device(front_in, child_block, child_rows, live_counts, column_map):
    rows_dev, cols_dev = front_in.shape
    owners, parts = lax.axis_size(ROW), lax.axis_size("col")
    chips = lax.axis_size(("z", "x"))
    count, child_width = child_block.shape
    capacity = count // owners
    core = lax.axis_index("core").astype(jnp.int32)
    col = lax.axis_index("col").astype(jnp.int32)
    is_root = (col == 0).astype(jnp.int32)
    halved = (f32(3 * PANELS // 2, BLOCK),) * 2
    local_cols = column_map % cols_dev

    step = capacity * (child_width // BLOCK) + 1
    sent = call(
        lambda *refs: pack_kernel(rows_dev, *refs), f32(owners * step, BLOCK), "pack", 1 << 20,
        child_block, child_rows.reshape(count // BLOCK, BLOCK), live_counts,
        ins=[HBM] * 3,
        vmem=56,
        scratch=[
            pltpu.VMEM((count, child_width), jnp.float32),
            pltpu.VMEM((count // BLOCK, BLOCK), jnp.int32),
            pltpu.VMEM((1, owners), jnp.int32),
            pltpu.SemaphoreType.DMA((3,)),
        ],
    )
    arrived = exchange(sent.reshape(owners, step, 1, BLOCK), ROW).reshape(owners * step, BLOCK)

    share = f32(rows_dev // parts, cols_dev)
    front, keep, send, *shares = call(
        lambda *refs: place_kernel(owners, *refs), [f32(rows_dev, cols_dev), *halved] + [share] * parts,
        "place", 4 << 30, front_in, arrived, local_cols.reshape(1, child_width), scalars=(core,),
        scratch=[pltpu.VMEM((3 * PANELS, BLOCK), jnp.float32)],
    )
    half = summed(keep, swapped(send))
    half, shares = lax.optimization_barrier((half, shares))
    far_first = sorted(range(1, parts), key=lambda k: -min(k, parts - k))
    sent_shares = [lax.ppermute(shares[k], "col", [(0, k)]) for k in far_first]
    grams = exchange(split_rows(half, chips), ("z", "x"))
    share_rows = rows_dev // parts * PANELS // BLOCK
    gram_rows = grams.shape[1]
    bundle = call(
        bundle_kernel, f32(parts, share_rows + gram_rows, BLOCK), "bundle", 1 << 20,
        grams, shares[0], *sent_shares, scalars=(is_root,), vmem=8,
    )
    bundle = exchange(bundle, "col")
    gram_share = call(
        gram_kernel, f32(chips, gram_rows, BLOCK), "gram_share", 1 << 20, bundle, vmem=6
    )
    own_gram = merge_rows(exchange(gram_share, ("z", "x")))
    other_gram = swapped(own_gram)

    panel, keep, send = call(
        product_kernel, (f32(rows_dev, PANELS),) + (f32(PANELS // 2, cols_dev),) * 2,
        "products", 2 << 30, front, bundle, scalars=(core,),
        scratch=[pltpu.VMEM((PANELS, cols_dev), jnp.float32)],
    )
    half = summed(keep, swapped(send))
    summands = exchange(split_rows(half, chips), ("z", "x"))

    block_shape = f32(PANELS // PIECES, 3 * PANELS // 2)
    upper = call(
        lambda *refs: factor_kernel(0, *refs), block_shape, "factor0", 1 << 30,
        own_gram, other_gram, scalars=(core,),
    )
    summands, upper = lax.optimization_barrier((summands, upper))
    own_sums = merge_rows(exchange(folded(summands, chips), ("z", "x")))
    lower, basis = call(
        last_factor_kernel, (block_shape, f32(rows_dev, PANELS)), "factor1", 12 << 30,
        own_gram, other_gram, panel, upper, scalars=(core,),
    )
    own_sums, basis = lax.optimization_barrier((own_sums, basis))
    other_sums = swapped(own_sums)
    whole = (rows_dev, cols_dev)
    ins = (upper, lower, own_sums, other_sums, basis, front)
    return call(
        lambda *refs: final_kernel(math.sqrt(rows_dev * owners), *refs),
        (f32(*whole), f32(PANELS, cols_dev)), "final", 4 << 30, *ins, scalars=(core, is_root),
        ins=[HBM] * len(ins), outs=(HBM, HBM), vmem=56,
        scratch=[pltpu.VMEM(x.shape, jnp.float32) for x in ins]
        + [pltpu.VMEM(whole, jnp.float32), pltpu.VMEM((PANELS, cols_dev), jnp.float32)]
        + [pltpu.SemaphoreType.DMA((9,))],
    )


def solution(mesh):
    row, col = mesh.shape["row"], mesh.shape["col"]
    fine = Mesh(mesh.devices.reshape(8, 4, row // 32, col), ROW + ("col",))
    return jax.shard_map(
        on_device,
        mesh=fine,
        in_specs=(P(ROW, "col"), P(ROW, "col"), P(ROW), P(ROW, None), P("col")),
        out_specs=(P(ROW, "col"), P(None, "col")),
        check_vma=False,
    )
```
